512 devices in a mesh: gx: 64 (over z, x), gy: 8 (over y, core).
Axes of the slice: x: 4, y: 4, z: 16, core: 2. Of those that a mesh axis runs over, the one named last changes fastest.
Arguments:
- positions: float32 [3, 131072], P(None, ('gx', 'gy')), may hold values from 0 to 128, as said below
- features: float32 [128, 131072], P(None, ('gx', 'gy')), may hold values from -6 to 6
- neighbours: int32 [12, 131072], P(None, ('gx', 'gy')), may hold values from 0 to 25, as said below
- up_weight: float32 [128, 128], replicated, may hold values from -0.5 to 0.5
- radial_in: float32 [64, 8], replicated, may hold values from -2 to 2
- radial_out: float32 [384, 64], replicated, may hold values from -0.75 to 0.75
- coupling: float32 [2, 128], replicated, may hold values from 0.5 to 2
- mix_weight: float32 [128, 128], replicated, may hold values from -0.5 to 0.5
- readout: float32 [128], replicated, may hold values from -0.5 to 0.5
- charge_weight: float32 [128], replicated, may hold values from -0.5 to 0.5
Outputs:
- forces: float32 [3, 131072], P(None, ('gx', 'gy'))
- energy: float32 [], replicated
The draws below stay inside these ranges and needn't reach their ends.
Inputs may be any that keep to these rules, and one draw needn't show every extreme that they name: `positions`: atom a of a domain, with place (p, r, s) as in the reference program, lies within 0.3 of p + 0.5 along the first dimension, within 0.6 of 2 r + 1 along the second, and within 0.3 * 8 of (s + 0.5) * 8 along the third. `neighbours`: the 12 codes of an atom differ from one another.
All inputs are finite; a program needn't handle non-finite values.
Results may differ from the reference program's by a relative error of at most 0.0003.
Values sent between devices are 32-bit elements; how exact they have to be, the bound alone decides.
No kernel may reach another device: no remote copies, remote signals or barrier semaphores. Data moves between devices by JAX's collectives and lax.ppermute only.
A program may use at most 64 MiB of HBM per device.

```python
import math
import jax
import jax.numpy as jnp
from jax import lax

C = 128
NB = 8
RH = 64
K = 12
NZ = 128
ATOM_DEV = 256
ATOMS = 131072
N_GX = 64
N_GY = 8


def draw_positions(key, part):
    key = jax.random.fold_in(key, 11)
    z_sites = ATOM_DEV // 16
    spacing = NZ / z_sites
    atom_index = jnp.arange(ATOMS, dtype=jnp.int32) % ATOM_DEV
    plane_index = (atom_index // (8 * z_sites)).astype(jnp.float32)
    row_index = (atom_index // z_sites % 8).astype(jnp.float32)
    site_index = (atom_index % z_sites).astype(jnp.float32)
    jitter = jax.random.uniform(key, (3, ATOMS), jnp.float32, -1.0, 1.0)
    return jnp.stack([plane_index + 0.5 + 0.3 * jitter[0], 2.0 * row_index + 1.0 + 0.6 * jitter[1], (site_index + 0.5 + 0.3 * jitter[2]) * spacing])


def draw_neighbours(key, part):
    key = jax.random.fold_in(key, 23)
    scores = jax.random.randint(key, (ATOMS, 26), 0, 1 << 20)
    scores = scores * 32 + jnp.arange(26, dtype=jnp.int32)[None, :]
    ranking = jnp.argsort(scores, axis=1, stable=True)
    return ranking[:, :K].astype(jnp.int32).T


def levels(stream_key, extent, pieces, smallest, high):
    factor_of = 1.0
    for position, parts in pieces:
        steps = jax.random.uniform(jax.random.fold_in(jax.random.fold_in(stream_key, 6), position), (parts,), jnp.float32, smallest / len(pieces), high / len(pieces))
        factor_of = factor_of * jnp.repeat(jnp.exp(steps), extent[position] // parts).reshape((-1,) + (1,) * (len(extent) - 1 - position))
    return factor_of


def gaussian(own_key, shape, scale, bound, cuts=(), kind=jnp.bfloat16):
    entries = jax.random.normal(own_key, shape, jnp.float32) * scale
    if len(cuts) > 0:
        entries = levels(own_key, shape, cuts, -0.22, 0.18) * entries
    return jnp.clip(entries, min=-bound, max=bound).astype(kind)


def setup_inputs(seed: int = 0) -> dict:
    keys = jax.random.split(jax.random.key(seed), 11)
    return {
        "positions": draw_positions(jax.random.fold_in(keys[10], 71), 0),
        "features": gaussian(keys[1], (C, ATOMS), 1.0, 6.0, ((1, 512),), jnp.float32),
        "neighbours": draw_neighbours(jax.random.fold_in(keys[10], 71), 0),
        "up_weight": gaussian(keys[3], (C, C), C ** -0.5, 0.5, (), jnp.float32),
        "radial_in": gaussian(keys[4], (RH, NB), NB ** -0.5, 2.0, (), jnp.float32),
        "radial_out": gaussian(keys[5], (3 * C, RH), RH ** -0.5, 0.75, (), jnp.float32),
        "coupling": jnp.clip(jax.random.uniform(keys[6], (2, C), jnp.float32, 0.5, 2.0), 0.5, 2.0),
        "mix_weight": gaussian(keys[7], (C, C), C ** -0.5, 0.5, (), jnp.float32),
        "readout": gaussian(keys[8], (C,), C ** -0.5, 0.5, (), jnp.float32),
        "charge_weight": gaussian(keys[9], (C,), C ** -0.5, 0.5, (), jnp.float32),
    }


highest = lax.Precision.HIGHEST
ewald_beta = 0.5

def lattice_offsets(codes):
    shifted = codes + (codes >= 13).astype(jnp.int32)
    return (shifted // 9 - 1, shifted // 3 % 3 - 1, shifted % 3 - 1)

def harmonics(unit_vec):
    along_x, along_y, along_z = (unit_vec[0], unit_vec[1], unit_vec[2])
    root_three = math.sqrt(3.0)
    root_five = math.sqrt(5.0)
    root_fifteen = math.sqrt(15.0)
    first_order = jnp.stack([root_three * along_x, root_three * along_y, root_three * along_z])
    second_order = jnp.stack([root_fifteen * along_x * along_y, root_fifteen * along_y * along_z, 0.5 * root_five * (3.0 * along_z * along_z - 1.0), root_fifteen * along_x * along_z, 0.5 * root_fifteen * (along_x * along_x - along_y * along_y)])
    return (first_order, second_order)

def radial_basis(distance, cutoff, basis_count):
    harmonic_order = jnp.arange(1, basis_count + 1, dtype=jnp.int32).astype(jnp.float32)[:, None]
    scaled = distance[None, :] / cutoff
    envelope = 1.0 - 28.0 * scaled ** 6 + 48.0 * scaled ** 7 - 21.0 * scaled ** 8
    return math.sqrt(2.0 / cutoff) * jnp.sin(harmonic_order * math.pi * scaled) / distance[None, :] * envelope

def interaction(ext_pos, ext_up, features, codes, radial_in, radial_out, coupling, mix_weight, z_cells):
    z_sites = ext_pos.shape[3]
    channels, atom_count = features.shape
    neighbour_count = codes.shape[0]
    atom_index = jnp.arange(atom_count, dtype=jnp.int32)
    plane_index = atom_index // (8 * z_sites)
    row_index = atom_index // z_sites % 8
    site_index = atom_index % z_sites
    step_x, step_y, step_z = lattice_offsets(codes)
    target_z = site_index[None, :] + step_z
    wrapped = (target_z >= z_sites).astype(jnp.int32) - (target_z < 0).astype(jnp.int32)
    target = ((plane_index[None, :] + step_x + 1) * 10 + row_index[None, :] + step_y + 1) * z_sites + target_z - wrapped * z_sites
    flat_target = target.reshape(-1)
    own_pos = ext_pos[:, 1:3, 1:9, :].reshape(3, atom_count)
    other_pos = jnp.take(ext_pos.reshape(3, -1), flat_target, axis=1).reshape(3, neighbour_count, atom_count)
    relative = other_pos - own_pos[:, None, :]
    relative = jnp.stack([relative[0], relative[1], relative[2] + wrapped.astype(jnp.float32) * z_cells])
    distance = jnp.sqrt(lax.optimization_barrier(jnp.sum(relative * relative, axis=0)))
    unit_vec = relative / distance[None]
    cutoff = 2.0 * z_cells / z_sites + 4.0
    basis = radial_basis(distance.reshape(-1), cutoff, radial_in.shape[1])
    hidden = jax.nn.silu(jnp.dot(radial_in, basis, precision=highest))
    radial = jnp.dot(radial_out, hidden, precision=highest).reshape(3, channels, neighbour_count, atom_count)
    neighbour_up = jnp.take(ext_up, flat_target, axis=1).reshape(channels, neighbour_count, atom_count)
    weighted = radial * neighbour_up[None]
    first_order, second_order = harmonics(unit_vec)
    scalar_part = lax.optimization_barrier(jnp.sum(weighted[0], axis=1)) / neighbour_count
    vector_part = jnp.einsum('ckn,mkn->mcn', weighted[1], first_order, precision=highest) / neighbour_count
    tensor_part = jnp.einsum('ckn,mkn->mcn', weighted[2], second_order, precision=highest) / neighbour_count
    product = scalar_part + coupling[0][:, None] * lax.optimization_barrier(jnp.sum(vector_part * vector_part, axis=0)) + coupling[1][:, None] * lax.optimization_barrier(jnp.sum(tensor_part * tensor_part, axis=0))
    return features + jnp.dot(mix_weight, product, precision=highest)

def spline_weights(fraction):
    remainder = 1.0 - fraction
    fraction_square = fraction * fraction
    fraction_cube = fraction_square * fraction
    return [remainder * remainder * remainder / 6.0, (3.0 * fraction_cube - 6.0 * fraction_square + 4.0) / 6.0, (-3.0 * fraction_cube + 3.0 * fraction_square + 3.0 * fraction + 1.0) / 6.0, fraction_cube / 6.0]

def ewald_kernel(index_x, index_y, index_z, length_x, length_y, length_z):
    squared = 0.0
    moduli = 1.0
    for wave_index, length in ((index_x, length_x), (index_y, length_y), (index_z, length_z)):
        folded = wave_index - length * (2 * wave_index >= length).astype(jnp.int32)
        wave_number = 2.0 * math.pi / length * folded.astype(jnp.float32)
        squared = squared + wave_number * wave_number
        moduli = moduli * (6.0 / (4.0 + 2.0 * jnp.cos(2.0 * math.pi / length * wave_index.astype(jnp.float32)))) ** 2
    anchor = (index_x == 0) & (index_y == 0) & (index_z == 0)
    safe_square = jnp.where(anchor, 1.0, squared)
    return jnp.where(anchor, 0.0, 4.0 * math.pi * jnp.exp(-safe_square / (4.0 * ewald_beta ** 2)) / safe_square * moduli)

def long_range(coords, charges, grid_x, grid_y):
    lengths = (grid_x, grid_y, NZ)
    cell_lists = []
    weight_lists = []
    for dimension in range(3):
        floored = jnp.floor(coords[dimension])
        base_index = floored.astype(jnp.int32)
        cell_lists.append([(base_index + spline_step - 1) % lengths[dimension] for spline_step in range(4)])
        weight_lists.append(spline_weights(coords[dimension] - floored))
    grid = jnp.zeros((grid_x, grid_y, NZ), jnp.float32)
    for first_step in range(4):
        for second_step in range(4):
            for third_step in range(4):
                grid = grid.at[cell_lists[0][first_step], cell_lists[1][second_step], cell_lists[2][third_step]].add(charges * weight_lists[0][first_step] * weight_lists[1][second_step] * weight_lists[2][third_step])
    spectrum = jnp.fft.fftn(grid)
    power = jnp.real(spectrum) ** 2 + jnp.imag(spectrum) ** 2
    kernel = ewald_kernel(jnp.arange(grid_x, dtype=jnp.int32)[:, None, None], jnp.arange(grid_y, dtype=jnp.int32)[None, :, None], jnp.arange(NZ, dtype=jnp.int32)[None, None, :], grid_x, grid_y, NZ)
    return jnp.sum(kernel * power) / (2.0 * grid_x * grid_y * NZ)

def reference(positions, features, neighbours, up_weight, radial_in, radial_out, coupling, mix_weight, readout, charge_weight):
    z_sites = ATOM_DEV // 16
    domains = N_GX * N_GY
    grid_x = 2 * N_GX
    grid_y = 16 * N_GY
    up_all = jnp.dot(up_weight, features, precision=highest)
    feature_blocks = jnp.moveaxis(features.reshape(C, domains, ATOM_DEV), 1, 0)
    code_blocks = jnp.moveaxis(neighbours.reshape(K, domains, ATOM_DEV), 1, 0)
    domain_index = jnp.arange(ATOMS, dtype=jnp.int32) // ATOM_DEV
    corner_x = (2 * (domain_index // N_GY)).astype(jnp.float32)
    corner_y = (16 * (domain_index % N_GY)).astype(jnp.float32)

    def blocks(array):
        return jnp.moveaxis(array.reshape(array.shape[0], N_GX, N_GY, 2, 8, z_sites), 0, 2)

    def one_domain(inputs):
        table_one, feature_one, code_one = inputs
        updated = interaction(table_one[:3], table_one[3:].reshape(C, -1), feature_one, code_one, radial_in, radial_out, coupling, mix_weight, float(NZ))
        return (jnp.dot(readout, updated, precision=highest), jnp.dot(charge_weight, updated, precision=highest))

    def total_energy(coords):
        packed = blocks(jnp.concatenate([coords, up_all], axis=0))
        lower_x = jnp.roll(packed[:, :, :, 1], 1, axis=0).at[:, :, 0].add(-2.0)
        upper_x = jnp.roll(packed[:, :, :, 0], -1, axis=0).at[:, :, 0].add(2.0)
        widened = jnp.stack([lower_x, packed[:, :, :, 0], packed[:, :, :, 1], upper_x], axis=3)
        lower_y = jnp.roll(widened[:, :, :, :, 7], 1, axis=1).at[:, :, 1].add(-16.0)
        upper_y = jnp.roll(widened[:, :, :, :, 0], -1, axis=1).at[:, :, 1].add(16.0)
        ghost_table = jnp.concatenate([lower_y[:, :, :, :, None], widened, upper_y[:, :, :, :, None]], axis=4)
        ghost_table = ghost_table.reshape(domains, C + 3, 4, 10, z_sites)
        site_energy, charges = lax.map(jax.checkpoint(one_domain), (ghost_table, feature_blocks, code_blocks))
        grid_coords = jnp.stack([coords[0] + corner_x, coords[1] + corner_y, coords[2]])
        return jnp.sum(site_energy) + long_range(grid_coords, charges.reshape(-1), grid_x, grid_y)
    energy, gradient = jax.value_and_grad(total_energy)(positions)
    return (-gradient, energy / ATOMS)
```

```python
import math

import jax
import jax.numpy as jnp
import numpy as np
from jax import lax
from jax.experimental import pallas as pl
from jax.experimental.pallas import tpu as pltpu
from jax.sharding import PartitionSpec as P

NZ = 128
N_GX = 64
N_GY = 8
K = 12
C = 128
RH = 64
NB = 8
ATOMS_ALL = 131072
ATOM = 256
EXT = 640
CUTOFF = 20.0
BETA = 0.5

PLANE0 = -1
PLANES = 5
ROW0 = -1
ROWS = 19
ROW_PAD = 24
SUM_ROW = 23
SUM_LANE = 16 * PLANES

highest = lax.Precision.HIGHEST
f32 = jnp.float32
bf16 = jnp.bfloat16


def real_basis(n):
    cell = np.arange(n)
    rows = [np.full(n, 1.0 / math.sqrt(n))]
    freq = [0]
    for m in range(1, n // 2):
        angle = 2.0 * math.pi / n * (m * cell % n)
        rows += [math.sqrt(2.0 / n) * np.cos(angle), math.sqrt(2.0 / n) * np.sin(angle)]
        freq += [m, m]
    rows.append(np.where(cell % 2 == 0, 1.0, -1.0) / math.sqrt(n))
    freq.append(n // 2)
    return np.stack(rows), np.array(freq)


def tables():
    basis, freq = real_basis(NZ)
    wave = 2.0 * math.pi / NZ * freq
    square = wave * wave
    gain = np.exp(-square / (4.0 * BETA**2)) * (6.0 / (4.0 + 2.0 * np.cos(wave))) ** 2

    plane = (2 * np.arange(N_GX)[None, :] + PLANE0 + np.arange(PLANES)[:, None]) % NZ
    x_in = np.concatenate([basis[:, plane[p]] for p in range(PLANES)], axis=0)
    x_out = np.concatenate([basis[:, plane[p]].T for p in range(PLANES)], axis=0)

    y_in = np.zeros((NZ, N_GY * ROW_PAD))
    for j in range(N_GY):
        for r in range(ROWS):
            y_in[:, j * ROW_PAD + r] = basis[:, (16 * j + ROW0 + r) % NZ]
        y_in[:, j * ROW_PAD + SUM_ROW] = 1.0

    x_side = np.zeros((NZ, NZ, 2))
    x_side[:, :, 0] = 4.0 * math.pi * gain[:, None]
    x_side[:, :, 1] = square[:, None]

    yz = np.zeros((N_GX * N_GY, 4, 128))
    for i in range(N_GX):
        for j in range(N_GY):
            z = slice(16 * j, 16 * j + 16)
            for half in range(2):
                y = i + 64 * half
                yz[i * N_GY + j, 2 * half, :16] = gain[y] * gain[z]
                yz[i * N_GY + j, 2 * half + 1, :16] = square[y] + square[z]
    as32 = lambda a: np.ascontiguousarray(a, dtype=np.float32)
    return {
        "z": as32(basis),
        "y_in": as32(y_in),
        "y_out": as32(y_in.T),
        "x_in": as32(x_in),
        "x_out": as32(x_out),
        "x_gain": as32(x_side[:, :, 0]),
        "x_square": as32(x_side[:, :, 1]),
        "yz": as32(yz),
    }


TABLES = tables()


def dot(a, b, precision=None):
    return jnp.dot(a, b, precision=precision, preferred_element_type=f32)


def dot_nt(a, b, precision=None):
    return lax.dot_general(
        a, b, (((1,), (1,)), ((), ())), precision=precision, preferred_element_type=f32
    )


def halves(x):
    high = x.astype(bf16).astype(f32)
    return high, x - high


def spline(f):
    g = 1.0 - f
    f2 = f * f
    f3 = f2 * f
    weights = [
        g * g * g / 6.0,
        (3.0 * f3 - 6.0 * f2 + 4.0) / 6.0,
        (-3.0 * f3 + 3.0 * f2 + 3.0 * f + 1.0) / 6.0,
        f3 / 6.0,
    ]
    slopes = [-0.5 * g * g, 1.5 * f2 - 2.0 * f, -1.5 * f2 + f + 0.5, 0.5 * f2]
    return weights, slopes


def spline_rows(u, first, rows, periodic):
    floor = jnp.floor(u)
    base = floor.astype(jnp.int32)
    weights, slopes = spline(u - floor)
    cell = lax.broadcasted_iota(jnp.int32, (rows, u.shape[1]), 0) + first
    table = jnp.zeros((rows, u.shape[1]), f32)
    slope_table = jnp.zeros((rows, u.shape[1]), f32)
    for step in range(4):
        target = base + (step - 1)
        if periodic:
            target = target & (rows - 1)
        hit = cell == target
        table = jnp.where(hit, weights[step], table)
        slope_table = jnp.where(hit, slopes[step], slope_table)
    return table, slope_table


def edge_targets(codes):
    shape = codes.shape
    e = codes + (codes >= 13).astype(jnp.int32)
    nine = (e >= 9).astype(jnp.int32) + (e >= 18).astype(jnp.int32)
    rest = e - 9 * nine
    three = (rest >= 3).astype(jnp.int32) + (rest >= 6).astype(jnp.int32)
    step_z = rest - 3 * three - 1
    n = lax.broadcasted_iota(jnp.int32, shape, 1)
    plane = (n >> 7) + nine
    row = ((n >> 4) & 7) + three - 1
    z = (n & 15) + step_z
    wrap = (z >= 16).astype(jnp.int32) - (z < 0).astype(jnp.int32)
    z = z - 16 * wrap
    target = jnp.where(
        row < 0,
        512 + plane * 16 + z,
        jnp.where(row > 7, 576 + plane * 16 + z, plane * 128 + row * 16 + z),
    )
    return target, wrap


def one_hot(target_ref, k):
    row = jnp.broadcast_to(target_ref[pl.ds(k, 1), :], (EXT, ATOM))
    column = lax.broadcasted_iota(jnp.int32, (EXT, ATOM), 0)
    return jnp.where(column == row, 1.0, 0.0).astype(bf16)


EDGE_SCRATCH = [
    pltpu.VMEM((136, EXT), f32),
    pltpu.VMEM((288, EXT), bf16),
    pltpu.VMEM((K, ATOM), jnp.int32),
    pltpu.VMEM((3, K, ATOM), f32),
    pltpu.VMEM((K, C, ATOM), f32),
    pltpu.VMEM((K, NB, ATOM), f32),
    pltpu.VMEM((K, NB, ATOM), f32),
    pltpu.VMEM((K, 8, 8, ATOM), f32),
    pltpu.VMEM((3 * C, 3 * RH), f32),
    pltpu.VMEM((K, 3 * C, ATOM), f32),
    pltpu.VMEM((9, C, ATOM), f32),
    pltpu.VMEM((8, C), f32),
]


def edges(left, own, right, low, high, codes, up_weight, radial_in, radial_out, scratch, slopes):
    (table, split, target_ref, near, up, basis, basis_slope, harm, weights, radial, sums, _) = (
        scratch
    )
    table[:, 0:128] = left[...]
    table[:, 128:384] = own[...]
    table[:, 384:512] = right[...]
    table[:, 512:576] = low[...]
    table[:, 576:640] = high[...]

    w_high, w_low = halves(up_weight[...])
    t_high, t_low = halves(table[0:C, :])
    t_high = t_high.astype(bf16)
    mapped = dot(w_high.astype(bf16), t_high)
    mapped = mapped + dot(w_high.astype(bf16), t_low.astype(bf16))
    mapped = mapped + dot(w_low.astype(bf16), t_high)
    m_high, m_low = halves(mapped)
    split[0:C, :] = m_high.astype(bf16)
    split[C : 2 * C, :] = m_low.astype(bf16)

    lane = lax.broadcasted_iota(jnp.int32, (8, EXT), 1)
    part = lax.broadcasted_iota(jnp.int32, (8, EXT), 0)
    plane = jnp.where(lane < 512, lane >> 7, (lane >> 4) & 3)
    shift_x = jnp.where(plane == 0, -2.0, jnp.where(plane == 3, 2.0, 0.0))
    shift_y = jnp.where(lane >= 576, 16.0, jnp.where(lane >= 512, -16.0, 0.0))
    places = table[C : C + 8, :] + jnp.where(
        part == 0, shift_x, jnp.where(part == 1, shift_y, 0.0)
    )
    p_high, p_rest = halves(places)
    p_mid, p_low = halves(p_rest)
    split[2 * C : 2 * C + 32, :] = jnp.concatenate(
        [p_high, p_mid, p_low, jnp.zeros_like(p_low)], axis=0
    ).astype(bf16)

    target, wrap = edge_targets(codes[...])
    target_ref[...] = target

    def gather(k, carry):
        found = dot(split[...], one_hot(target_ref, k))
        up[k] = found[0:C] + found[C : 2 * C]
        place = found[256:264] + found[264:272] + found[272:280]
        for c in range(3):
            near[c, pl.ds(k, 1), :] = place[c : c + 1]
        return carry

    lax.fori_loop(0, K, gather, 0)

    rel_x = near[0] - own[C : C + 1, :]
    rel_y = near[1] - own[C + 1 : C + 2, :]
    rel_z = near[2] - own[C + 2 : C + 3, :] + wrap.astype(f32) * float(NZ)
    square = rel_x * rel_x + rel_y * rel_y + rel_z * rel_z
    dist = jnp.sqrt(square)
    inv = 1.0 / dist
    ux, uy, uz = rel_x * inv, rel_y * inv, rel_z * inv
    r3, r5, r15 = math.sqrt(3.0), math.sqrt(5.0), math.sqrt(15.0)
    harmonic = [
        r3 * ux,
        r3 * uy,
        r3 * uz,
        r15 * ux * uy,
        r15 * uy * uz,
        0.5 * r5 * (3.0 * uz * uz - 1.0),
        r15 * ux * uz,
        0.5 * r15 * (ux * ux - uy * uy),
    ]
    for m in range(8):
        for k in range(K):
            harm[k, m] = jnp.broadcast_to(harmonic[m][k : k + 1, :], (8, ATOM))

    t = dist * (1.0 / CUTOFF)
    t2 = t * t
    t4 = t2 * t2
    t5 = t4 * t
    t6 = t4 * t2
    envelope = 1.0 - t6 * (28.0 - t * (48.0 - 21.0 * t))
    theta = math.pi * t
    sines, cosines = {1: jnp.sin(theta)}, {1: jnp.cos(theta)}
    for b in range(2, NB + 1):
        i, j = (b + 1) // 2, b // 2
        sines[b] = sines[i] * cosines[j] + cosines[i] * sines[j]
        cosines[b] = cosines[i] * cosines[j] - sines[i] * sines[j]
    scale = math.sqrt(2.0 / CUTOFF)
    shape = scale * envelope * inv
    if slopes:
        envelope_slope = (-168.0 / CUTOFF) * t5 * (1.0 - t) * (1.0 - t)
        shape_slope = scale * inv * (envelope_slope - envelope * inv)
    for b in range(1, NB + 1):
        value = sines[b] * shape
        for k in range(K):
            basis[k, b - 1 : b, :] = value[k : k + 1, :]
        if slopes:
            value = (b * math.pi / CUTOFF) * cosines[b] * shape + sines[b] * shape_slope
            for k in range(K):
                basis_slope[k, b - 1 : b, :] = value[k : k + 1, :]

    o_high, o_low = halves(radial_out[...])
    weights[:, 0:RH] = o_high
    weights[:, RH : 2 * RH] = o_high
    weights[:, 2 * RH : 3 * RH] = o_low
    wide = weights[...].astype(bf16)

    def layered(hidden):
        s_high, s_low = halves(hidden)
        return dot(wide, jnp.concatenate([s_high, s_low, s_high], axis=0).astype(bf16))

    for k in range(K):
        before = dot(radial_in[...], basis[k], highest)
        gate = jax.nn.sigmoid(before)
        radial[k] = layered(before * gate)
        if slopes:
            before_slope = dot(radial_in[...], basis_slope[k], highest)
            gate_slope = gate * (1.0 + before * (1.0 - gate))
            slopes[0][k] = layered(gate_slope * before_slope)

    def accumulate(step, carry):
        c0 = pl.multiple_of((step % 16) * 8, 8)
        n0 = pl.multiple_of((step // 16) * 128, 128)
        total = [jnp.zeros((8, 128), f32) for _ in range(9)]
        for k in range(K):
            u = up[k, pl.ds(c0, 8), pl.ds(n0, 128)]
            total[0] += radial[k, pl.ds(c0, 8), pl.ds(n0, 128)] * u
            first = radial[k, pl.ds(c0 + C, 8), pl.ds(n0, 128)] * u
            second = radial[k, pl.ds(c0 + 2 * C, 8), pl.ds(n0, 128)] * u
            for m in range(8):
                total[1 + m] += (first if m < 3 else second) * harm[k, m, :, pl.ds(n0, 128)]
        for m in range(9):
            sums[m, pl.ds(c0, 8), pl.ds(n0, 128)] = total[m]
        return carry

    lax.fori_loop(0, 32, accumulate, 0)
    return dist, inv, ux, uy, uz


def readout_rows(readout, charge_weight, mix_weight, rows):
    rows[...] = jnp.zeros_like(rows)
    rows[0:1, :] = readout[...]
    rows[1:2, :] = charge_weight[...]
    return rows[...], dot(rows[...], mix_weight[...], highest)


def charges_kernel(
    left, own, right, low, high, codes, up_weight, radial_in, radial_out, coupling, mix_weight,
    readout, charge_weight, z_table, spread, charge_out, *scratch,
):
    own_pos = own[C : C + 8, :]
    weights_x, _ = spline_rows(own_pos[0:1], PLANE0, 8, False)
    weights_y, _ = spline_rows(own_pos[1:2], ROW0, ROW_PAD, False)
    weights_z, _ = spline_rows(own_pos[2:3], 0, NZ, True)
    waves_z = dot(z_table[...], weights_z, highest)

    edges(
        left, own, right, low, high, codes, up_weight, radial_in, radial_out, scratch, None
    )
    sums = scratch[10]
    direct, mixed = readout_rows(readout, charge_weight, mix_weight, scratch[11])
    inv_k = 1.0 / K
    first = sum(sums[m] * sums[m] for m in range(1, 4))
    second = sum(sums[m] * sums[m] for m in range(4, 9))
    outs = dot(direct, own[0:C, :], highest)
    outs = outs + dot(mixed * inv_k, sums[0], highest)
    outs = outs + dot(mixed * coupling[0:1, :] * inv_k**2, first, highest)
    outs = outs + dot(mixed * coupling[1:2, :] * inv_k**2, second, highest)
    site = jnp.sum(outs[0:1, :])
    charge = outs[1:2, :]
    charge_out[...] = charge

    charged = weights_y * charge
    planes = [dot_nt(charged * weights_x[p : p + 1], waves_z, highest) for p in range(PLANES)]
    lane = lax.broadcasted_iota(jnp.int32, (ROW_PAD, 128), 1)
    row = lax.broadcasted_iota(jnp.int32, (ROW_PAD, 128), 0)
    extra = jnp.where((lane == SUM_LANE) & (row == SUM_ROW), site, 0.0)
    for g in range(N_GY):
        part = extra
        for p in range(PLANES):
            moved = pltpu.roll(planes[p], (16 * (p - g)) % 128, 1)
            part = jnp.where((lane >> 4) == p, moved, part)
        spread[g] = part


def y_in_kernel(rows, table, out):
    waves = dot(table[...], rows[...].reshape(N_GY * ROW_PAD, 128), highest)
    out[:, 0, :] = waves[0:64]
    out[:, 1, :] = waves[64:128]


def x_kernel(planes, x_in, x_out, x_gain, x_square, yz, out):
    sides = jnp.concatenate([planes[:, 0, :], planes[:, 1, :]], axis=1)
    site = jnp.sum(planes[:, 0, SUM_LANE : SUM_LANE + 1])
    waves = dot(x_in[...], sides, highest)
    filtered = []
    energy = site * (1.0 / (N_GX * N_GY))
    for half in range(2):
        total = waves[0:128, 128 * half : 128 * half + 128]
        for p in range(1, PLANES):
            block = waves[128 * p : 128 * p + 128, 128 * half : 128 * half + 128]
            total = total + pltpu.roll(block, (128 - 16 * p) % 128, 1)
        square = x_square[...] + yz[0, 2 * half + 1 : 2 * half + 2, :]
        anchor = square == 0.0
        kernel = jnp.where(
            anchor,
            0.0,
            x_gain[...] * yz[0, 2 * half : 2 * half + 1, :] / jnp.where(anchor, 1.0, square),
        )
        shaped = kernel * total
        energy = energy + 0.5 * jnp.sum(shaped * total)
        filtered.append(shaped)
    back = dot(x_out[...], jnp.concatenate(filtered, axis=1), highest)
    lane = lax.broadcasted_iota(jnp.int32, (64, 128), 1)
    for half in range(2):
        total = jnp.where(lane == SUM_LANE, energy, 0.0) if half == 0 else jnp.zeros((64, 128), f32)
        for p in range(PLANES):
            block = back[64 * p : 64 * p + 64, 128 * half : 128 * half + 128]
            moved = pltpu.roll(block, 16 * p, 1) if p else block
            total = total + moved
        out[:, half, :] = total


def y_out_kernel(waves, table, out):
    both = jnp.concatenate([waves[:, 0, :], waves[:, 1, :]], axis=0)
    out[...] = dot(table[...], both, highest).reshape(N_GY, ROW_PAD, 128)


def slopes_kernel(
    left, own, right, low, high, codes, up_weight, radial_in, radial_out, coupling, mix_weight,
    readout, charge_weight, pulls, *scratch,
):
    edge_scratch, (radial_slope, columns, gathered) = scratch[:12], scratch[12:]
    dist, inv, ux, uy, uz = edges(
        left, own, right, low, high, codes, up_weight, radial_in, radial_out, edge_scratch,
        (radial_slope,),
    )
    up, harm, radial, sums = (edge_scratch[i] for i in (4, 7, 9, 10))
    _, mixed = readout_rows(readout, charge_weight, mix_weight, edge_scratch[11])
    part = lax.broadcasted_iota(jnp.int32, (8, C), 0)
    inv_k = 1.0 / K
    rows = mixed * inv_k
    rows = jnp.where(part == 2, coupling[0:1, :] * (2.0 * inv_k), rows)
    rows = jnp.where(part == 3, coupling[1:2, :] * (2.0 * inv_k), rows)
    standing = rows.T
    for i in range(4):
        columns[i] = jnp.broadcast_to(standing[:, i : i + 1], (C, 128))
    for m in range(1, 9):
        for half in range(2):
            lanes = slice(128 * half, 128 * half + 128)
            sums[m, :, lanes] = sums[m, :, lanes] * columns[2 if m < 4 else 3]

    def pull(step, carry):
        k = step // 2
        n0 = pl.multiple_of((step % 2) * 128, 128)
        spots = pl.ds(n0, 128)
        total = [jnp.zeros((8, 128), f32) for _ in range(18)]
        shapes = [harm[k, m, :, spots] for m in range(8)]
        for block in range(16):
            c0 = 8 * block
            u = up[k, c0 : c0 + 8, spots]
            along = [sums[1 + m, c0 : c0 + 8, spots] for m in range(8)]
            turn_1 = sum(along[m] * shapes[m] for m in range(3))
            turn_2 = sum(along[m] * shapes[m] for m in range(3, 8))
            stretch = u * (
                radial_slope[k, c0 : c0 + 8, spots]
                + radial_slope[k, C + c0 : C + c0 + 8, spots] * turn_1
                + radial_slope[k, 2 * C + c0 : 2 * C + c0 + 8, spots] * turn_2
            )
            first = radial[k, C + c0 : C + c0 + 8, spots] * u
            second = radial[k, 2 * C + c0 : 2 * C + c0 + 8, spots] * u
            for w in range(2):
                weight = columns[w, c0 : c0 + 8, :]
                total[9 * w] += weight * stretch
                first_w = weight * first
                second_w = weight * second
                for m in range(8):
                    total[9 * w + 1 + m] += (first_w if m < 3 else second_w) * along[m]
        sums_18 = [jnp.sum(total[i], axis=0, keepdims=True) for i in range(18)]
        gathered[k, :, spots] = jnp.concatenate(sums_18 + [jnp.zeros((6, 128), f32)], axis=0)
        return carry

    lax.fori_loop(0, 2 * K, pull, 0)

    r3, r5, r15 = math.sqrt(3.0), math.sqrt(5.0), math.sqrt(15.0)
    for w in range(2):
        g = [
            jnp.concatenate([gathered[k, 9 * w + i : 9 * w + i + 1, :] for k in range(K)], axis=0)
            for i in range(9)
        ]
        vx = r3 * g[1] + r15 * (uy * g[4] + uz * g[7] + ux * g[8])
        vy = r3 * g[2] + r15 * (ux * g[4] + uz * g[5] - uy * g[8])
        vz = r3 * g[3] + r15 * (uy * g[5] + ux * g[7]) + (3.0 * r5) * uz * g[6]
        radial_part = g[0] - (vx * ux + vy * uy + vz * uz) * inv
        pulls[3 * w] = radial_part * ux + vx * inv
        pulls[3 * w + 1] = radial_part * uy + vy * inv
        pulls[3 * w + 2] = radial_part * uz + vz * inv


def final_kernel(potential, positions, codes, charge, z_table, pulls, out, energy_out, target_ref):
    target, _ = edge_targets(codes[...])
    target_ref[...] = target
    weights_x, slopes_x = spline_rows(positions[0:1, :], PLANE0, 8, False)
    weights_y, slopes_y = spline_rows(positions[1:2, :], ROW0, ROW_PAD, False)
    weights_z, slopes_z = spline_rows(positions[2:3, :], 0, NZ, True)
    waves = dot(z_table[...], jnp.concatenate([weights_z, slopes_z], axis=1), highest)

    lane = lax.broadcasted_iota(jnp.int32, (ROW_PAD, 128), 1)
    phi = jnp.zeros((1, ATOM), f32)
    slope = [phi, phi, phi]
    energy = jnp.zeros((1, 1), f32)
    for g in range(N_GY):
        energy = energy + potential[g, SUM_ROW : SUM_ROW + 1, SUM_LANE : SUM_LANE + 1]
    energy_out[...] = energy * (1.0 / ATOMS_ALL)
    for p in range(PLANES):
        plane = jnp.zeros((ROW_PAD, 128), f32)
        for g in range(N_GY):
            amount = (16 * (g - p)) % 128
            moved = pltpu.roll(potential[g], amount, 1) if amount else potential[g]
            plane = jnp.where((lane >> 4) == g, moved, plane)
        felt = dot(plane, waves, highest)
        here = felt[:, 0:ATOM]
        by_y = jnp.sum(here * weights_y, axis=0, keepdims=True)
        phi = phi + by_y * weights_x[p : p + 1]
        slope[0] = slope[0] + by_y * slopes_x[p : p + 1]
        by_y = jnp.sum(here * slopes_y, axis=0, keepdims=True)
        slope[1] = slope[1] + by_y * weights_x[p : p + 1]
        by_y = jnp.sum(felt[:, ATOM:] * weights_y, axis=0, keepdims=True)
        slope[2] = slope[2] + by_y * weights_x[p : p + 1]

    total = [pulls[c] + phi * pulls[3 + c] for c in range(3)]
    out[...] = jnp.zeros_like(out)
    table = jnp.zeros((16, EXT), f32)
    for k in range(K):
        rows = jnp.concatenate(
            [total[c][k : k + 1, :] for c in range(3)] + [jnp.zeros((5, ATOM), f32)], axis=0
        )
        high, low = halves(rows)
        both = jnp.concatenate([high, low], axis=0).astype(bf16)
        table = table + dot_nt(both, one_hot(target_ref, k))
    out[...] = table[0:8] + table[8:16]
    for c in range(3):
        own = charge[...] * slope[c] - jnp.sum(total[c], axis=0, keepdims=True)
        out[c : c + 1, 128:384] = out[c : c + 1, 128:384] + own


def call(kernel, outs, scratch, flops, *args):
    return pl.pallas_call(
        kernel,
        out_shape=outs,
        scratch_shapes=scratch,
        compiler_params=pltpu.CompilerParams(vmem_limit_bytes=48 * 1024 * 1024),
        cost_estimate=pl.CostEstimate(flops=flops, bytes_accessed=2000000, transcendentals=0),
    )(*args)


def passed_along(array, axis, by):
    devices = lax.axis_size(axis)
    return lax.ppermute(array, axis, [(i, (i + by) % devices) for i in range(devices)])


def struct(*shape):
    return jax.ShapeDtypeStruct(shape, f32)


def shards(
    positions, features, neighbours, up_weight, radial_in, radial_out, coupling, mix_weight,
    readout, charge_weight,
):
    table = {name: jnp.asarray(value) for name, value in TABLES.items()}
    own = jnp.concatenate([features, positions, jnp.zeros((5, ATOM), f32)], axis=0)
    left = passed_along(own[:, 128:256], "gx", 1)
    right = passed_along(own[:, 0:128], "gx", -1)
    low = passed_along(
        jnp.concatenate([left[:, 112:], own[:, 112:128], own[:, 240:], right[:, 112:]], axis=1),
        "gy",
        1,
    )
    high = passed_along(
        jnp.concatenate([left[:, :16], own[:, 0:16], own[:, 128:144], right[:, :16]], axis=1),
        "gy",
        -1,
    )
    edge_args = (left, own, right, low, high, neighbours, up_weight, radial_in, radial_out)
    weight_args = (coupling, mix_weight, readout.reshape(1, C), charge_weight.reshape(1, C))

    spread, charge = call(
        charges_kernel,
        (struct(N_GY, ROW_PAD, 128), struct(1, ATOM)),
        EDGE_SCRATCH,
        10**9,
        *edge_args,
        *weight_args,
        table["z"],
    )
    rows = lax.all_to_all(spread, "gy", split_axis=0, concat_axis=0, tiled=True)
    waves = call(y_in_kernel, struct(N_GX, 2, 128), [], 10**7, rows, table["y_in"])
    planes = lax.all_to_all(waves, "gx", split_axis=0, concat_axis=0, tiled=True)
    device = lax.axis_index("gx") * N_GY + lax.axis_index("gy")
    yz = lax.dynamic_slice(table["yz"], (device, 0, 0), (1, 4, 128))
    waves = call(
        x_kernel,
        struct(N_GX, 2, 128),
        [],
        10**7,
        planes,
        table["x_in"],
        table["x_out"],
        table["x_gain"],
        table["x_square"],
        yz,
    )
    waves = lax.all_to_all(waves, "gx", split_axis=0, concat_axis=0, tiled=True)
    rows = call(y_out_kernel, struct(N_GY, ROW_PAD, 128), [], 10**7, waves, table["y_out"])
    potential = lax.all_to_all(rows, "gy", split_axis=0, concat_axis=0, tiled=True)

    pulls = call(
        slopes_kernel,
        struct(6, K, ATOM),
        EDGE_SCRATCH
        + [
            pltpu.VMEM((K, 3 * C, ATOM), f32),
            pltpu.VMEM((4, C, 128), f32),
            pltpu.VMEM((K, 24, ATOM), f32),
        ],
        4 * 10**9,
        *edge_args,
        *weight_args,
    )
    gradient, energy = call(
        final_kernel,
        (struct(8, EXT), struct(1, 1)),
        [pltpu.VMEM((K, ATOM), jnp.int32)],
        10**9,
        potential,
        positions,
        neighbours,
        charge,
        table["z"],
        pulls,
    )
    gradient = gradient[:3]
    from_high = passed_along(gradient[:, 512:576], "gy", -1)
    from_low = passed_along(gradient[:, 576:640], "gy", 1)
    main = gradient[:, :512].reshape(3, 4, 8, 16)
    main = main.at[:, :, 7].add(from_high.reshape(3, 4, 16))
    main = main.at[:, :, 0].add(from_low.reshape(3, 4, 16))
    main = main.reshape(3, 4, 128)
    from_right = passed_along(main[:, 0], "gx", -1)
    from_left = passed_along(main[:, 3], "gx", 1)
    forces = -jnp.concatenate([main[:, 1] + from_left, main[:, 2] + from_right], axis=1)
    return (forces, energy.reshape(()))


def solution(mesh):
    placed = (P(None, ("gx", "gy")),) * 3 + (P(),) * 7
    return jax.shard_map(
        shards, mesh=mesh, in_specs=placed, out_specs=(P(None, ("gx", "gy")), P()), check_vma=False
    )
```

```python
import functools
import math

import jax
import jax.numpy as jnp
import ml_dtypes
import numpy as np
from jax import lax
from jax.experimental import pallas as pl
from jax.experimental.pallas import tpu as pltpu
from jax.sharding import PartitionSpec as P

NZ = 128
N_GX = 64
N_GY = 8
K = 12
HALF = K // 2
C = 128
RH = 64
NB = 8
ATOMS_ALL = 131072
ATOM = 256
EXT = 640
CUTOFF = 20.0
BETA = 0.5

PLANE0 = -2
PLANES = 7
OWN_PLANES = range(1, 6)
ROW0 = -3
ROWS = 23
ROW_PAD = 24
SUM_ROW = 23
SUM_LANE = 16 * PLANES

highest = lax.Precision.HIGHEST
f32 = jnp.float32
bf16 = jnp.bfloat16


def real_basis(n):
    cell = np.arange(n)
    rows = [np.full(n, 1.0 / math.sqrt(n))]
    freq = [0]
    for m in range(1, n // 2):
        angle = 2.0 * math.pi / n * (m * cell % n)
        rows += [math.sqrt(2.0 / n) * np.cos(angle), math.sqrt(2.0 / n) * np.sin(angle)]
        freq += [m, m]
    rows.append(np.where(cell % 2 == 0, 1.0, -1.0) / math.sqrt(n))
    freq.append(n // 2)
    return np.stack(rows), np.array(freq)


def tables():
    basis, freq = real_basis(NZ)
    wave = 2.0 * math.pi / NZ * freq
    square = wave * wave
    gain = np.exp(-square / (4.0 * BETA**2)) * (6.0 / (4.0 + 2.0 * np.cos(wave))) ** 2

    plane = (2 * np.arange(N_GX)[None, :] + PLANE0 + np.arange(PLANES)[:, None]) % NZ
    x_in = np.concatenate([basis[:, plane[p]] for p in OWN_PLANES], axis=0)
    x_out = np.concatenate([basis[:, plane[p]].T for p in range(PLANES)], axis=0)

    y_in = np.zeros((NZ, N_GY * ROW_PAD))
    for j in range(N_GY):
        for r in range(ROWS):
            y_in[:, j * ROW_PAD + r] = basis[:, (16 * j + ROW0 + r) % NZ]
        y_in[:, j * ROW_PAD + SUM_ROW] = 1.0

    x_side = np.zeros((NZ, NZ, 2))
    x_side[:, :, 0] = 4.0 * math.pi * gain[:, None]
    x_side[:, :, 1] = square[:, None]

    yz = np.zeros((N_GX * N_GY, 4, 128))
    for i in range(N_GX):
        for j in range(N_GY):
            z = slice(16 * j, 16 * j + 16)
            for half in range(2):
                y = i + 64 * half
                yz[i * N_GY + j, 2 * half, :16] = gain[y] * gain[z]
                yz[i * N_GY + j, 2 * half + 1, :16] = square[y] + square[z]
    as32 = lambda a: np.ascontiguousarray(a, dtype=np.float32)

    def split(a):
        high = as32(a).astype(ml_dtypes.bfloat16)
        low = (as32(a) - high.astype(np.float32)).astype(ml_dtypes.bfloat16)
        return np.concatenate([high, high, low], axis=1)

    return {
        "z": as32(basis),
        "y_in": split(y_in),
        "y_out": split(y_in.T),
        "x_in": split(x_in),
        "x_out": split(x_out),
        "x_gain": as32(x_side[:, :, 0]),
        "x_square": as32(x_side[:, :, 1]),
        "yz": as32(yz),
    }


TABLES = tables()


def dot(a, b, precision=None):
    return jnp.dot(a, b, precision=precision, preferred_element_type=f32)


def dot_nt(a, b, precision=None):
    return lax.dot_general(
        a, b, (((1,), (1,)), ((), ())), precision=precision, preferred_element_type=f32
    )


def halves(x):
    high = x.astype(bf16).astype(f32)
    return high, x - high


def layered(wide, x):
    high, low = halves(x)
    return dot(wide[...], jnp.concatenate([high, low, high], axis=0).astype(bf16))


def spread_out(value, lane):
    high, rest = halves(jnp.full(lane.shape, value, f32))
    mid, low = halves(rest)
    return jnp.where(
        lane == SUM_LANE,
        high,
        jnp.where(lane == SUM_LANE + 1, mid, jnp.where(lane == SUM_LANE + 2, low, 0.0)),
    )


def spline(f):
    g = 1.0 - f
    f2 = f * f
    f3 = f2 * f
    weights = [
        g * g * g / 6.0,
        (3.0 * f3 - 6.0 * f2 + 4.0) / 6.0,
        (-3.0 * f3 + 3.0 * f2 + 3.0 * f + 1.0) / 6.0,
        f3 / 6.0,
    ]
    slopes = [-0.5 * g * g, 1.5 * f2 - 2.0 * f, -1.5 * f2 + f + 0.5, 0.5 * f2]
    return weights, slopes


def spline_rows(u, first, rows, periodic):
    floor = jnp.floor(u)
    base = floor.astype(jnp.int32)
    weights, slopes = spline(u - floor)
    cell = lax.broadcasted_iota(jnp.int32, (rows, u.shape[1]), 0) + first
    table = jnp.zeros((rows, u.shape[1]), f32)
    slope_table = jnp.zeros((rows, u.shape[1]), f32)
    for step in range(4):
        target = base + (step - 1)
        if periodic:
            target = target & (rows - 1)
        hit = cell == target
        table = jnp.where(hit, weights[step], table)
        slope_table = jnp.where(hit, slopes[step], slope_table)
    return table, slope_table


def offsets(codes):
    e = codes + (codes >= 13).astype(jnp.int32)
    nine = (e >= 9).astype(jnp.int32) + (e >= 18).astype(jnp.int32)
    rest = e - 9 * nine
    three = (rest >= 3).astype(jnp.int32) + (rest >= 6).astype(jnp.int32)
    return nine, three, rest - 3 * three - 1


def own_targets(codes):
    nine, three, step_z = offsets(codes)
    n = lax.broadcasted_iota(jnp.int32, codes.shape, 1)
    inner = n < 512
    plane = jnp.where(inner, n >> 7, (n >> 4) & 3) + nine - 2
    row = jnp.where(inner, (n >> 4) & 7, jnp.where(n < 576, -1, 8)) + three - 1
    z = ((n & 15) + step_z) & 15
    here = (plane >= 0) & (plane <= 1) & (row >= 0) & (row <= 7)
    return jnp.where(here, plane * 128 + row * 16 + z, -1)


def edge_targets(codes):
    nine, three, step_z = offsets(codes)
    n = lax.broadcasted_iota(jnp.int32, codes.shape, 1)
    plane = (n >> 7) + nine
    row = ((n >> 4) & 7) + three - 1
    z = (n & 15) + step_z
    wrap = (z >= 16).astype(jnp.int32) - (z < 0).astype(jnp.int32)
    z = z - 16 * wrap
    target = jnp.where(
        row < 0,
        512 + plane * 16 + z,
        jnp.where(row > 7, 576 + plane * 16 + z, plane * 128 + row * 16 + z),
    )
    return target, wrap


def one_hot(target_ref, k, columns):
    lanes = target_ref.shape[1]
    row = jnp.broadcast_to(target_ref[k : k + 1, :], (columns, lanes))
    column = lax.broadcasted_iota(jnp.int32, (columns, lanes), 0)
    return jnp.where(column == row, 1.0, 0.0).astype(bf16)


def beside(x):
    high, low = halves(x)
    return jnp.concatenate([high, high, low], axis=1).astype(bf16)


def prepare_kernel(
    own, coupling, mix_weight, readout, charge_weight, up_weight, radial_in, radial_out, z_table,
    waves_out, columns_out, up_wide, in_wide, out_wide, rows,
):
    weights_z, _ = spline_rows(own[C + 2 : C + 3, :], 0, NZ, True)
    waves_out[...] = beside(dot(z_table[...], weights_z, highest))

    rows[...] = jnp.zeros_like(rows)
    rows[0:1, :] = readout[...]
    rows[1:2, :] = charge_weight[...]
    mixed = dot(rows[...], mix_weight[...], highest) * (1.0 / K)
    for w, direct in enumerate((readout, charge_weight)):
        row = mixed[w : w + 1]
        rows[4 * w : 4 * w + 1, :] = row
        rows[4 * w + 1 : 4 * w + 2, :] = row * coupling[0:1, :] * (1.0 / K)
        rows[4 * w + 2 : 4 * w + 3, :] = row * coupling[1:2, :] * (1.0 / K)
        rows[4 * w + 3 : 4 * w + 4, :] = direct[...]
    standing = rows[...].T
    for i in range(8):
        columns_out[i] = jnp.broadcast_to(standing[:, i : i + 1], (C, 128))
    rows[0:2, :] = coupling[...] * (2.0 / K)
    standing = rows[...].T
    for i in range(2):
        columns_out[8 + i] = jnp.broadcast_to(standing[:, i : i + 1], (C, 128))

    up_wide[...] = beside(up_weight[...])
    out_wide[...] = beside(radial_out[...].T)
    inner = radial_in[...].T
    column = lax.broadcasted_iota(jnp.int32, (NB, 8 * NB), 1)
    wave = lax.broadcasted_iota(jnp.int32, (NB, 8 * NB), 0)
    picks = [jnp.where(column == 8 * wave + k, 1.0, 0.0) for k in range(HALF)]
    in_wide[...] = beside(jnp.concatenate([dot(inner, p, highest) for p in picks], axis=0))


def slot(k):
    return 8 * (k // HALF) + k % HALF


def geometry(rel_x, rel_y, rel_z, harm, basis, basis_slope):
    square = rel_x * rel_x + rel_y * rel_y + rel_z * rel_z
    dist = jnp.sqrt(square)
    inv = 1.0 / dist
    ux, uy, uz = rel_x * inv, rel_y * inv, rel_z * inv
    r3, r5, r15 = math.sqrt(3.0), math.sqrt(5.0), math.sqrt(15.0)
    harmonic = [
        r3 * ux,
        r3 * uy,
        r3 * uz,
        r15 * ux * uy,
        r15 * uy * uz,
        0.5 * r5 * (3.0 * uz * uz - 1.0),
        r15 * ux * uz,
        0.5 * r15 * (ux * ux - uy * uy),
    ]
    for m in range(8):
        harm[m] = harmonic[m]

    t = dist * (1.0 / CUTOFF)
    t2 = t * t
    t4 = t2 * t2
    t5 = t4 * t
    t6 = t4 * t2
    envelope = 1.0 - t6 * (28.0 - t * (48.0 - 21.0 * t))
    theta = math.pi * t
    sines, cosines = {1: jnp.sin(theta)}, {1: jnp.cos(theta)}
    for b in range(2, NB + 1):
        i, j = (b + 1) // 2, b // 2
        sines[b] = sines[i] * cosines[j] + cosines[i] * sines[j]
        cosines[b] = cosines[i] * cosines[j] - sines[i] * sines[j]
    scale = math.sqrt(2.0 / CUTOFF)
    shape = scale * envelope * inv
    if basis_slope is not None:
        envelope_slope = (-168.0 / CUTOFF) * t5 * (1.0 - t) * (1.0 - t)
        shape_slope = scale * inv * (envelope_slope - envelope * inv)
    for b in range(1, NB + 1):
        value = sines[b] * shape
        for half in range(value.shape[0] // 8):
            basis[half, 8 * b - 8 : 8 * b, :] = value[8 * half : 8 * half + 8]
        if basis_slope is not None:
            basis_slope[8 * b - 8 : 8 * b, :] = (
                (b * math.pi / CUTOFF) * cosines[b] * shape + sines[b] * shape_slope
            )
    return inv, ux, uy, uz


CHARGE_SCRATCH = [
    pltpu.VMEM((136, EXT), f32),
    pltpu.VMEM((288, EXT), bf16),
    pltpu.VMEM((16, ATOM), jnp.int32),
    pltpu.VMEM((2, 8 * NB, ATOM), f32),
    pltpu.VMEM((8, 16, ATOM), f32),
    pltpu.VMEM((K, 3 * C, ATOM), f32),
    pltpu.VMEM((K, C, ATOM), f32),
    pltpu.SemaphoreType.DMA((1,)),
]


def charges_kernel(
    left, own, right, low, high, codes, up_wide, in_wide, out_wide, columns, waves_z,
    spread, charge_out, rel, places_out, along, kept,
    table, split, target_ref, basis, harm, radial, up, sems,
):
    own_pos = own[C : C + 8, :]
    weights_x, _ = spline_rows(own_pos[0:1], PLANE0, 8, False)
    weights_y, _ = spline_rows(own_pos[1:2], ROW0, ROW_PAD, False)

    table[:, 0:128] = left[...]
    table[:, 128:384] = own[...]
    table[:, 384:512] = right[...]
    table[:, 512:576] = low[...]
    table[:, 576:640] = high[...]

    mapped = layered(up_wide, table[0:C, :])
    m_high, m_low = halves(mapped)
    split[0:C, :] = m_high.astype(bf16)
    split[C : 2 * C, :] = m_low.astype(bf16)

    lane = lax.broadcasted_iota(jnp.int32, (8, EXT), 1)
    part = lax.broadcasted_iota(jnp.int32, (8, EXT), 0)
    plane = jnp.where(lane < 512, lane >> 7, (lane >> 4) & 3)
    shift_x = jnp.where(plane == 0, -2.0, jnp.where(plane == 3, 2.0, 0.0))
    shift_y = jnp.where(lane >= 576, 16.0, jnp.where(lane >= 512, -16.0, 0.0))
    places = table[C : C + 8, :] + jnp.where(
        part == 0, shift_x, jnp.where(part == 1, shift_y, 0.0)
    )
    places_out[...] = places
    p_high, p_rest = halves(places)
    p_mid, p_low = halves(p_rest)
    split[2 * C : 2 * C + 32, :] = jnp.concatenate(
        [p_high, p_mid, p_low, jnp.zeros_like(p_low)], axis=0
    ).astype(bf16)

    padded = jnp.concatenate(
        [codes[0:HALF, :], codes[0:2, :], codes[HALF:K, :], codes[0:2, :]], axis=0
    )
    target, wrap = edge_targets(padded)
    target_ref[...] = target
    for k in range(K):
        found = dot(split[...], one_hot(target_ref, slot(k), EXT))
        up[k] = found[0:C] + found[C : 2 * C]
        place = found[256:264] + found[264:272] + found[272:280]
        for c in range(3):
            rel[c, slot(k) : slot(k) + 1, :] = place[c : c + 1]

    keep_up = pltpu.make_async_copy(up, kept, sems.at[0])
    keep_up.start()

    rel_x = rel[0] - own_pos[0:1]
    rel_y = rel[1] - own_pos[1:2]
    rel_z = rel[2] - own_pos[2:3] + wrap.astype(f32) * float(NZ)
    spare = (lax.broadcasted_iota(jnp.int32, (16, ATOM), 0) & 7) >= HALF
    rel_x, rel_y, rel_z = (jnp.where(spare, 1.0, x) for x in (rel_x, rel_y, rel_z))
    rel[0], rel[1], rel[2] = rel_x, rel_y, rel_z
    geometry(rel_x, rel_y, rel_z, harm, basis, None)

    for half in range(2):
        before = layered(in_wide, basis[half])
        hidden = before * jax.nn.sigmoid(before)
        for k in range(HALF):
            radial[HALF * half + k] = layered(out_wide, hidden[RH * k : RH * k + RH])

    charge = []
    site = jnp.zeros((8, 128), f32)
    for half in range(2):
        lanes = slice(128 * half, 128 * half + 128)

        def accumulate(step, carry):
            c0 = pl.multiple_of(step * 8, 8)
            block = pl.ds(c0, 8)
            total = [jnp.zeros((8, 128), f32) for _ in range(9)]
            for k in range(K):
                u = up[k, block, lanes]
                total[0] += radial[k, block, lanes] * u
                first = radial[k, pl.ds(c0 + C, 8), lanes] * u
                second = radial[k, pl.ds(c0 + 2 * C, 8), lanes] * u
                for m in range(8):
                    total[1 + m] += (
                        first if m < 3 else second
                    ) * harm[m, slot(k) : slot(k) + 1, lanes]
            for m in range(8):
                along[m, block, lanes] = total[1 + m] * columns[8 if m < 3 else 9, block, :]
            first = sum(total[m] * total[m] for m in range(1, 4))
            second = sum(total[m] * total[m] for m in range(4, 9))
            feature = own[block, lanes]
            return tuple(
                carry[w]
                + columns[4 * w, block, :] * total[0]
                + columns[4 * w + 1, block, :] * first
                + columns[4 * w + 2, block, :] * second
                + columns[4 * w + 3, block, :] * feature
                for w in range(2)
            )

        zero = jnp.zeros((8, 128), f32)
        sites, charges = lax.fori_loop(0, 16, accumulate, (zero, zero))
        site = site + sites
        charge.append(jnp.sum(charges, axis=0, keepdims=True))
    charge = jnp.concatenate(charge, axis=1)
    charge_out[...] = charge

    charged = weights_y * charge
    planes = jnp.concatenate([charged * weights_x[p : p + 1] for p in OWN_PLANES], axis=0)
    top, rest = halves(planes)
    planes = dot_nt(jnp.concatenate([top, rest, top], axis=1).astype(bf16), waves_z[...])
    lane = lax.broadcasted_iota(jnp.int32, (ROW_PAD, 128), 1)
    row = lax.broadcasted_iota(jnp.int32, (ROW_PAD, 128), 0)
    extra = jnp.where(row == SUM_ROW, spread_out(jnp.sum(site), lane), 0.0)
    for g in range(N_GY):
        part = extra
        for i, p in enumerate(OWN_PLANES):
            amount = (16 * (p - g)) % 128
            moved = planes[ROW_PAD * i : ROW_PAD * i + ROW_PAD]
            moved = pltpu.roll(moved, amount, 1) if amount else moved
            part = jnp.where((lane >> 4) == p, moved, part)
        spread[g] = part
    keep_up.wait()


def y_in_kernel(rows, table, out):
    waves = layered(table, rows[...].reshape(N_GY * ROW_PAD, 128))
    out[:, 0, :] = waves[0:64]
    out[:, 1, :] = waves[64:128]


def x_kernel(planes, x_in, x_out, x_gain, x_square, yz, out):
    sides = jnp.concatenate([planes[:, 0, :], planes[:, 1, :]], axis=1)
    site = jnp.sum(planes[:, 0, SUM_LANE : SUM_LANE + 3])
    waves = layered(x_in, sides)
    filtered = []
    energy = site * (1.0 / (N_GX * N_GY))
    for half in range(2):
        total = jnp.zeros((128, 128), f32)
        for i, p in enumerate(OWN_PLANES):
            block = waves[128 * i : 128 * i + 128, 128 * half : 128 * half + 128]
            total = total + pltpu.roll(block, (128 - 16 * p) % 128, 1)
        square = x_square[...] + yz[0, 2 * half + 1 : 2 * half + 2, :]
        anchor = square == 0.0
        kernel = jnp.where(
            anchor,
            0.0,
            x_gain[...] * yz[0, 2 * half : 2 * half + 1, :] / jnp.where(anchor, 1.0, square),
        )
        shaped = kernel * total
        energy = energy + 0.5 * jnp.sum(shaped * total)
        filtered.append(shaped)
    back = layered(x_out, jnp.concatenate(filtered, axis=1))
    lane = lax.broadcasted_iota(jnp.int32, (64, 128), 1)
    for half in range(2):
        total = spread_out(energy, lane) if half == 0 else jnp.zeros((64, 128), f32)
        for p in range(PLANES):
            block = back[64 * p : 64 * p + 64, 128 * half : 128 * half + 128]
            moved = pltpu.roll(block, 16 * p, 1) if p else block
            total = total + moved
        out[:, half, :] = total


def y_out_kernel(waves, table, out):
    both = jnp.concatenate([waves[:, 0, :], waves[:, 1, :]], axis=0)
    out[...] = layered(table, both).reshape(N_GY, ROW_PAD, 128)


SLOPE_SCRATCH = [
    pltpu.VMEM((1, 8 * NB, ATOM), f32),
    pltpu.VMEM((8 * NB, ATOM), f32),
    pltpu.VMEM((8, 8, ATOM), f32),
    pltpu.VMEM((HALF, 3 * C, ATOM), f32),
    pltpu.VMEM((HALF, 3 * C, ATOM), f32),
    pltpu.VMEM((HALF, 24, ATOM), f32),
    pltpu.VMEM((HALF, C, ATOM), f32),
    pltpu.SemaphoreType.DMA((1,)),
]


def slopes_kernel(
    k0, rel, kept, along, codes, in_wide, out_wide, columns, pulls,
    basis, basis_slope, harm, radial, radial_slope, gathered, up, sems,
):
    fetch_up = pltpu.make_async_copy(kept.at[k0 : k0 + HALF], up, sems.at[0])
    fetch_up.start()
    first = slot(k0)
    inv, ux, uy, uz = geometry(
        *(rel[c, first : first + 8, :] for c in range(3)), harm, basis, basis_slope
    )
    before = layered(in_wide, basis[0])
    before_slope = layered(in_wide, basis_slope[...])
    gate = jax.nn.sigmoid(before)
    hidden = before * gate
    hidden_slope = gate * (1.0 + before * (1.0 - gate)) * before_slope
    for k in range(HALF):
        radial[k] = layered(out_wide, hidden[RH * k : RH * k + RH])
        radial_slope[k] = layered(out_wide, hidden_slope[RH * k : RH * k + RH])

    fetch_up.wait()
    for half in range(2):
        spots = slice(128 * half, 128 * half + 128)

        for k in range(HALF):
            total = [jnp.zeros((8, 128), f32) for _ in range(18)]
            shapes = [
                jnp.broadcast_to(harm[m, k : k + 1, spots], (8, 128)) for m in range(8)
            ]
            for block in range(16):
                c0 = 8 * block
                rows = [slice(c0 + C * i, c0 + C * i + 8) for i in range(3)]
                u = up[k, rows[0], spots]
                turn = [along[m, rows[0], spots] for m in range(8)]
                turn_1 = sum(turn[m] * shapes[m] for m in range(3))
                turn_2 = sum(turn[m] * shapes[m] for m in range(3, 8))
                stretch = u * (
                    radial_slope[k, rows[0], spots]
                    + radial_slope[k, rows[1], spots] * turn_1
                    + radial_slope[k, rows[2], spots] * turn_2
                )
                first = radial[k, rows[1], spots] * u
                second = radial[k, rows[2], spots] * u
                for w in range(2):
                    weight = columns[4 * w, rows[0], :]
                    total[9 * w] += weight * stretch
                    first_w = weight * first
                    second_w = weight * second
                    for m in range(8):
                        total[9 * w + 1 + m] += (first_w if m < 3 else second_w) * turn[m]
            sums = [jnp.sum(total[i], axis=0, keepdims=True) for i in range(18)]
            gathered[k, :, spots] = jnp.concatenate(sums + [jnp.zeros((6, 128), f32)], axis=0)

    r3, r5, r15 = math.sqrt(3.0), math.sqrt(5.0), math.sqrt(15.0)
    for w in range(2):
        g = [
            jnp.concatenate(
                [gathered[k, i : i + 1, :] for k in range(HALF)] + [jnp.zeros((2, ATOM), f32)],
                axis=0,
            )
            for i in range(9 * w, 9 * w + 9)
        ]
        vx = r3 * g[1] + r15 * (uy * g[4] + uz * g[7] + ux * g[8])
        vy = r3 * g[2] + r15 * (ux * g[4] + uz * g[5] - uy * g[8])
        vz = r3 * g[3] + r15 * (uy * g[5] + ux * g[7]) + (3.0 * r5) * uz * g[6]
        radial_part = g[0] - (vx * ux + vy * uy + vz * uz) * inv
        for c, (v, along_c) in enumerate(((vx, ux), (vy, uy), (vz, uz))):
            first = 8 * (3 * w + c)
            pulls[first : first + HALF, :] = (radial_part * along_c + v * inv)[0:HALF]
            spare = codes[k0 + 2 * c : k0 + 2 * c + 2, :].astype(f32)
            pulls[first + HALF : first + 8, :] = spare if w == 0 else jnp.zeros_like(spare)


def reach_kernel(pulls_0, pulls_1, places, z_table, out, lower, upper):
    weights, slopes = spline_rows(places[2:3, :], 0, NZ, True)
    both = jnp.concatenate([weights, slopes[:, 128:384]], axis=1)
    out[...] = dot(z_table[...], both, highest)
    for half, pulls in enumerate((pulls_0, pulls_1)):
        rows = slice(48 * half, 48 * half + 48)
        lower[rows, :] = pulls[:, 0:128]
        upper[rows, :] = pulls[:, 128:256]


def final_kernel(
    potential, places, charge, waves, left, lower, upper, right, low, high, forces, energy_out,
    pulls, target_ref,
):
    pulls[:, 0:128] = left[...]
    pulls[:, 128:256] = lower[...]
    pulls[:, 256:384] = upper[...]
    pulls[:, 384:512] = right[...]
    pulls[:, 512:576] = low[...]
    pulls[:, 576:640] = high[...]
    codes = [
        pulls[48 * half + 8 * c + HALF : 48 * half + 8 * c + 8, :]
        for half in range(2)
        for c in range(3)
    ]
    codes = jnp.concatenate(codes, axis=0)
    target_ref[...] = own_targets(codes.astype(jnp.int32))

    mine = slice(128, 384)
    weights_x, slopes_x = spline_rows(places[0:1, :], PLANE0, 8, False)
    weights_y, slopes_y = spline_rows(places[1:2, :], ROW0, ROW_PAD, False)
    lane = lax.broadcasted_iota(jnp.int32, (ROW_PAD, 128), 1)
    energy = jnp.zeros((1, 3), f32)
    for g in range(N_GY):
        energy = energy + potential[g, SUM_ROW : SUM_ROW + 1, SUM_LANE : SUM_LANE + 3]
    energy_out[...] = jnp.sum(energy, axis=1, keepdims=True) * (1.0 / ATOMS_ALL)
    planes = []
    for p in range(PLANES):
        plane = jnp.zeros((ROW_PAD, 128), f32)
        for g in range(N_GY):
            amount = (16 * (g - p)) % 128
            moved = pltpu.roll(potential[g], amount, 1) if amount else potential[g]
            plane = jnp.where((lane >> 4) == g, moved, plane)
        planes.append(plane)
    felt = dot(jnp.concatenate(planes, axis=0), waves[...], highest)
    phi = jnp.zeros((1, EXT), f32)
    slope = [jnp.zeros((1, ATOM), f32)] * 3
    for p in range(PLANES):
        here = felt[ROW_PAD * p : ROW_PAD * p + ROW_PAD, 0:EXT]
        by_y = jnp.sum(here * weights_y, axis=0, keepdims=True)
        phi = phi + by_y * weights_x[p : p + 1]
        slope[0] = slope[0] + by_y[:, mine] * slopes_x[p : p + 1, mine]
        by_y = jnp.sum(here[:, mine] * slopes_y[:, mine], axis=0, keepdims=True)
        slope[1] = slope[1] + by_y * weights_x[p : p + 1, mine]
        here = felt[ROW_PAD * p : ROW_PAD * p + ROW_PAD, EXT:]
        by_y = jnp.sum(here * weights_y[:, mine], axis=0, keepdims=True)
        slope[2] = slope[2] + by_y * weights_x[p : p + 1, mine]

    total = [
        [
            pulls[i + 8 * c : i + 8 * c + 8, :] + phi * pulls[i + 24 + 8 * c : i + 32 + 8 * c, :]
            for c in range(3)
        ]
        for i in (0, 48)
    ]
    table = jnp.zeros((16, ATOM), f32)
    for k in range(K):
        rows = jnp.concatenate(
            [total[k // HALF][c][k % HALF : k % HALF + 1, :] for c in range(3)]
            + [jnp.zeros((5, EXT), f32)],
            axis=0,
        )
        top, rest = halves(rows)
        both = jnp.concatenate([top, rest], axis=0).astype(bf16)
        table = table + dot_nt(both, one_hot(target_ref, k, ATOM))
    for c in range(3):
        forces[c : c + 1, :] = (
            jnp.sum(total[0][c][0:HALF, mine] + total[1][c][0:HALF, mine], axis=0, keepdims=True)
            - table[c : c + 1]
            - table[8 + c : 9 + c]
            - charge[...] * slope[c]
        )


def call(kernel, outs, scratch, flops, *args, far_in=(), far_out=(), mib=8):
    args = [
        pltpu.with_memory_space_constraint(x, pltpu.HBM) if i in far_in else x
        for i, x in enumerate(args)
    ]
    near, far = pl.BlockSpec(memory_space=pltpu.VMEM), pl.BlockSpec(memory_space=pltpu.HBM)
    out_specs = near
    if isinstance(outs, tuple):
        out_specs = tuple(far if i in far_out else near for i in range(len(outs)))
    return pl.pallas_call(
        kernel,
        out_shape=outs,
        in_specs=[far if i in far_in else near for i in range(len(args))],
        out_specs=out_specs,
        scratch_shapes=scratch,
        compiler_params=pltpu.CompilerParams(vmem_limit_bytes=mib * 1024 * 1024),
        cost_estimate=pl.CostEstimate(flops=flops, bytes_accessed=2000000, transcendentals=0),
    )(*args)


def passed_along(array, axis, by):
    devices = lax.axis_size(axis)
    return lax.ppermute(array, axis, [(i, (i + by) % devices) for i in range(devices)])


def ghosts(lower, upper):
    left = passed_along(upper, "gx", 1)
    right = passed_along(lower, "gx", -1)
    planes = (left, lower, upper, right)
    low = passed_along(jnp.concatenate([x[:, 112:] for x in planes], axis=1), "gy", 1)
    high = passed_along(jnp.concatenate([x[:, :16] for x in planes], axis=1), "gy", -1)
    return left, right, low, high


def struct(*shape, dtype=f32):
    return jax.ShapeDtypeStruct(shape, dtype)


def shards(
    positions, features, neighbours, up_weight, radial_in, radial_out, coupling, mix_weight,
    readout, charge_weight,
):
    table = {name: jnp.asarray(value) for name, value in TABLES.items()}
    own = jnp.concatenate([features, positions, jnp.zeros((5, ATOM), f32)], axis=0)
    left, right, low, high = ghosts(own[:, 0:128], own[:, 128:256])
    waves_z, columns, up_wide, in_wide, out_wide = call(
        prepare_kernel,
        (
            struct(NZ, 3 * ATOM, dtype=bf16),
            struct(10, C, 128),
            struct(C, 3 * C, dtype=bf16),
            struct(HALF * RH, 24 * NB, dtype=bf16),
            struct(3 * C, 3 * RH, dtype=bf16),
        ),
        [pltpu.VMEM((8, C), f32)],
        10**8,
        own,
        coupling,
        mix_weight,
        readout.reshape(1, C),
        charge_weight.reshape(1, C),
        up_weight,
        radial_in.T,
        radial_out.T,
        table["z"],
    )
    device = lax.axis_index("gx") * N_GY + lax.axis_index("gy")
    yz = lax.dynamic_slice(table["yz"], (device, 0, 0), (1, 4, 128))

    spread, charge, rel, places, along, kept = call(
        charges_kernel,
        (
            struct(N_GY, ROW_PAD, 128),
            struct(1, ATOM),
            struct(3, 16, ATOM),
            struct(8, EXT),
            struct(8, C, ATOM),
            pltpu.HBM((K, C, ATOM), f32),
        ),
        CHARGE_SCRATCH,
        10**9,
        left,
        own,
        right,
        low,
        high,
        neighbours,
        up_wide,
        in_wide,
        out_wide,
        columns,
        waves_z,
        far_out=(5,),
        mib=28,
    )
    spread, yz = lax.optimization_barrier((spread, yz))

    def pulls_of(k0, kept):
        return call(
            functools.partial(slopes_kernel, k0),
            struct(48, ATOM),
            SLOPE_SCRATCH,
            2 * 10**9,
            rel,
            kept,
            along,
            neighbours,
            in_wide,
            out_wide,
            columns,
            far_in=(1,),
            mib=28,
        )

    rows = lax.all_to_all(spread, "gy", split_axis=0, concat_axis=0, tiled=True)
    pulls_0 = pulls_of(0, kept)
    rows, pulls_0 = lax.optimization_barrier((rows, pulls_0))
    waves = call(y_in_kernel, struct(N_GX, 2, 128), [], 10**7, rows, table["y_in"])
    waves, kept = lax.optimization_barrier((waves, kept))
    planes = lax.all_to_all(waves, "gx", split_axis=0, concat_axis=0, tiled=True)
    pulls_1 = pulls_of(HALF, kept)
    planes, pulls_1 = lax.optimization_barrier((planes, pulls_1))
    waves = call(
        x_kernel,
        struct(N_GX, 2, 128),
        [],
        10**7,
        planes,
        table["x_in"],
        table["x_out"],
        table["x_gain"],
        table["x_square"],
        yz,
    )
    waves, pulls_0, pulls_1 = lax.optimization_barrier((waves, pulls_0, pulls_1))
    reach, lower, upper = call(
        reach_kernel,
        (struct(NZ, EXT + ATOM), struct(96, 128), struct(96, 128)),
        [],
        10**9,
        pulls_0,
        pulls_1,
        places,
        table["z"],
    )
    waves = lax.all_to_all(waves, "gx", split_axis=0, concat_axis=0, tiled=True)
    left, right, low, high = ghosts(lower, upper)
    rows = call(y_out_kernel, struct(N_GY, ROW_PAD, 128), [], 10**7, waves, table["y_out"])
    potential = lax.all_to_all(rows, "gy", split_axis=0, concat_axis=0, tiled=True)
    forces, energy = call(
        final_kernel,
        (struct(3, ATOM), struct(1, 1)),
        [pltpu.VMEM((96, EXT), f32), pltpu.VMEM((K, EXT), jnp.int32)],
        10**9,
        potential,
        places,
        charge,
        reach,
        left,
        lower,
        upper,
        right,
        low,
        high,
    )
    return (forces, energy.reshape(()))


def solution(mesh):
    placed = (P(None, ("gx", "gy")),) * 3 + (P(),) * 7
    return jax.shard_map(
        shards, mesh=mesh, in_specs=placed, out_specs=(P(None, ("gx", "gy")), P()), check_vma=False
    )
```

```python
import functools
import math

import jax
import jax.numpy as jnp
import ml_dtypes
import numpy as np
from jax import lax
from jax.experimental import pallas as pl
from jax.experimental.pallas import tpu as pltpu
from jax.sharding import PartitionSpec as P

NZ = 128
N_GX = 64
N_GY = 8
K = 12
HALF = K // 2
C = 128
RH = 64
NB = 8
ATOMS_ALL = 131072
ATOM = 256
EXT = 640
CUTOFF = 20.0
BETA = 0.5

PLANE0 = -2
PLANES = 7
OWN_PLANES = range(1, 6)
ROW0 = -3
ROWS = 23
ROW_PAD = 24
SUM_ROW = 23
SUM_LANE = 16 * PLANES

highest = lax.Precision.HIGHEST
f32 = jnp.float32
bf16 = jnp.bfloat16


def real_basis(n):
    cell = np.arange(n)
    rows = [np.full(n, 1.0 / math.sqrt(n))]
    freq = [0]
    for m in range(1, n // 2):
        angle = 2.0 * math.pi / n * (m * cell % n)
        rows += [math.sqrt(2.0 / n) * np.cos(angle), math.sqrt(2.0 / n) * np.sin(angle)]
        freq += [m, m]
    rows.append(np.where(cell % 2 == 0, 1.0, -1.0) / math.sqrt(n))
    freq.append(n // 2)
    return np.stack(rows), np.array(freq)


def tables():
    basis, freq = real_basis(NZ)
    wave = 2.0 * math.pi / NZ * freq
    square = wave * wave
    gain = np.exp(-square / (4.0 * BETA**2)) * (6.0 / (4.0 + 2.0 * np.cos(wave))) ** 2

    plane = (2 * np.arange(N_GX)[None, :] + PLANE0 + np.arange(PLANES)[:, None]) % NZ
    x_in = np.concatenate([basis[:, plane[p]] for p in OWN_PLANES], axis=0)
    x_out = np.concatenate([basis[:, plane[p]].T for p in range(PLANES)], axis=0)

    y_in = np.zeros((NZ, N_GY * ROW_PAD))
    for j in range(N_GY):
        for r in range(ROWS):
            y_in[:, j * ROW_PAD + r] = basis[:, (16 * j + ROW0 + r) % NZ]
        y_in[:, j * ROW_PAD + SUM_ROW] = 1.0

    x_side = np.zeros((NZ, NZ, 2))
    x_side[:, :, 0] = 4.0 * math.pi * gain[:, None]
    x_side[:, :, 1] = square[:, None]

    yz = np.zeros((N_GX * N_GY, 4, 128))
    for i in range(N_GX):
        for j in range(N_GY):
            z = slice(16 * j, 16 * j + 16)
            for half in range(2):
                y = i + 64 * half
                yz[i * N_GY + j, 2 * half, :16] = gain[y] * gain[z]
                yz[i * N_GY + j, 2 * half + 1, :16] = square[y] + square[z]
    as32 = lambda a: np.ascontiguousarray(a, dtype=np.float32)

    def split(a):
        high = as32(a).astype(ml_dtypes.bfloat16)
        low = (as32(a) - high.astype(np.float32)).astype(ml_dtypes.bfloat16)
        return np.concatenate([high, high, low], axis=1)

    return {
        "z": as32(basis),
        "y_in": split(y_in),
        "y_out": split(y_in.T),
        "x_in": split(x_in),
        "x_out": split(x_out),
        "x_gain": as32(x_side[:, :, 0]),
        "x_square": as32(x_side[:, :, 1]),
        "yz": as32(yz),
    }


TABLES = tables()


def dot(a, b, precision=None):
    return jnp.dot(a, b, precision=precision, preferred_element_type=f32)


def dot_nt(a, b, precision=None):
    return lax.dot_general(
        a, b, (((1,), (1,)), ((), ())), precision=precision, preferred_element_type=f32
    )


def halves(x):
    high = x.astype(bf16).astype(f32)
    return high, x - high


def layered(wide, x):
    high, low = halves(x)
    return dot(wide[...], jnp.concatenate([high, low, high], axis=0).astype(bf16))


def spread_out(value, lane):
    high, rest = halves(jnp.full(lane.shape, value, f32))
    mid, low = halves(rest)
    return jnp.where(
        lane == SUM_LANE,
        high,
        jnp.where(lane == SUM_LANE + 1, mid, jnp.where(lane == SUM_LANE + 2, low, 0.0)),
    )


def spline(f):
    g = 1.0 - f
    f2 = f * f
    f3 = f2 * f
    weights = [
        g * g * g / 6.0,
        (3.0 * f3 - 6.0 * f2 + 4.0) / 6.0,
        (-3.0 * f3 + 3.0 * f2 + 3.0 * f + 1.0) / 6.0,
        f3 / 6.0,
    ]
    slopes = [-0.5 * g * g, 1.5 * f2 - 2.0 * f, -1.5 * f2 + f + 0.5, 0.5 * f2]
    return weights, slopes


def spline_rows(u, first, rows, periodic):
    floor = jnp.floor(u)
    base = floor.astype(jnp.int32)
    weights, slopes = spline(u - floor)
    cell = lax.broadcasted_iota(jnp.int32, (rows, u.shape[1]), 0) + first
    table = jnp.zeros((rows, u.shape[1]), f32)
    slope_table = jnp.zeros((rows, u.shape[1]), f32)
    for step in range(4):
        target = base + (step - 1)
        if periodic:
            target = target & (rows - 1)
        hit = cell == target
        table = jnp.where(hit, weights[step], table)
        slope_table = jnp.where(hit, slopes[step], slope_table)
    return table, slope_table


def offsets(codes):
    e = codes + (codes >= 13).astype(jnp.int32)
    nine = (e >= 9).astype(jnp.int32) + (e >= 18).astype(jnp.int32)
    rest = e - 9 * nine
    three = (rest >= 3).astype(jnp.int32) + (rest >= 6).astype(jnp.int32)
    return nine, three, rest - 3 * three - 1


def own_targets(codes):
    nine, three, step_z = offsets(codes)
    n = lax.broadcasted_iota(jnp.int32, codes.shape, 1)
    inner = n < 512
    plane = jnp.where(inner, n >> 7, (n >> 4) & 3) + nine - 2
    row = jnp.where(inner, (n >> 4) & 7, jnp.where(n < 576, -1, 8)) + three - 1
    z = ((n & 15) + step_z) & 15
    here = (plane >= 0) & (plane <= 1) & (row >= 0) & (row <= 7)
    return jnp.where(here, plane * 128 + row * 16 + z, -1)


def edge_targets(codes):
    nine, three, step_z = offsets(codes)
    n = lax.broadcasted_iota(jnp.int32, codes.shape, 1)
    plane = (n >> 7) + nine
    row = ((n >> 4) & 7) + three - 1
    z = (n & 15) + step_z
    wrap = (z >= 16).astype(jnp.int32) - (z < 0).astype(jnp.int32)
    z = z - 16 * wrap
    target = jnp.where(
        row < 0,
        512 + plane * 16 + z,
        jnp.where(row > 7, 576 + plane * 16 + z, plane * 128 + row * 16 + z),
    )
    return target, wrap


def one_hot(target_ref, k, columns):
    lanes = target_ref.shape[1]
    row = jnp.broadcast_to(target_ref[k : k + 1, :], (columns, lanes))
    column = lax.broadcasted_iota(jnp.int32, (columns, lanes), 0)
    return jnp.where(column == row, 1.0, 0.0).astype(bf16)


def beside(x):
    high, low = halves(x)
    return jnp.concatenate([high, high, low], axis=1).astype(bf16)


def prepare_kernel(
    own, coupling, mix_weight, readout, charge_weight, up_weight, radial_in, radial_out, z_table,
    waves_out, columns_out, up_wide, in_wide, out_wide, rows,
):
    weights_z, _ = spline_rows(own[C + 2 : C + 3, :], 0, NZ, True)
    waves_out[...] = beside(dot(z_table[...], weights_z, highest))

    rows[...] = jnp.zeros_like(rows)
    rows[0:1, :] = readout[...]
    rows[1:2, :] = charge_weight[...]
    mixed = dot(rows[...], mix_weight[...], highest) * (1.0 / K)
    for w, direct in enumerate((readout, charge_weight)):
        row = mixed[w : w + 1]
        rows[4 * w : 4 * w + 1, :] = row
        rows[4 * w + 1 : 4 * w + 2, :] = row * coupling[0:1, :] * (1.0 / K)
        rows[4 * w + 2 : 4 * w + 3, :] = row * coupling[1:2, :] * (1.0 / K)
        rows[4 * w + 3 : 4 * w + 4, :] = direct[...]
    standing = rows[...].T
    for i in range(8):
        columns_out[i] = jnp.broadcast_to(standing[:, i : i + 1], (C, 128))
    rows[0:2, :] = coupling[...] * (2.0 / K)
    standing = rows[...].T
    for i in range(2):
        columns_out[8 + i] = jnp.broadcast_to(standing[:, i : i + 1], (C, 128))

    up_wide[...] = beside(up_weight[...])
    out_wide[...] = beside(radial_out[...].T)
    inner = radial_in[...].T
    column = lax.broadcasted_iota(jnp.int32, (NB, 8 * NB), 1)
    wave = lax.broadcasted_iota(jnp.int32, (NB, 8 * NB), 0)
    picks = [jnp.where(column == 8 * wave + k, 1.0, 0.0) for k in range(HALF)]
    in_wide[...] = beside(jnp.concatenate([dot(inner, p, highest) for p in picks], axis=0))


def slot(k):
    return 8 * (k // HALF) + k % HALF


def geometry(rel_x, rel_y, rel_z, harm, basis, basis_slope):
    square = rel_x * rel_x + rel_y * rel_y + rel_z * rel_z
    dist = jnp.sqrt(square)
    inv = 1.0 / dist
    ux, uy, uz = rel_x * inv, rel_y * inv, rel_z * inv
    r3, r5, r15 = math.sqrt(3.0), math.sqrt(5.0), math.sqrt(15.0)
    harmonic = [
        r3 * ux,
        r3 * uy,
        r3 * uz,
        r15 * ux * uy,
        r15 * uy * uz,
        0.5 * r5 * (3.0 * uz * uz - 1.0),
        r15 * ux * uz,
        0.5 * r15 * (ux * ux - uy * uy),
    ]
    for m in range(8):
        harm[m] = harmonic[m]

    t = dist * (1.0 / CUTOFF)
    t2 = t * t
    t4 = t2 * t2
    t5 = t4 * t
    t6 = t4 * t2
    envelope = 1.0 - t6 * (28.0 - t * (48.0 - 21.0 * t))
    theta = math.pi * t
    sines, cosines = {1: jnp.sin(theta)}, {1: jnp.cos(theta)}
    for b in range(2, NB + 1):
        i, j = (b + 1) // 2, b // 2
        sines[b] = sines[i] * cosines[j] + cosines[i] * sines[j]
        cosines[b] = cosines[i] * cosines[j] - sines[i] * sines[j]
    scale = math.sqrt(2.0 / CUTOFF)
    shape = scale * envelope * inv
    if basis_slope is not None:
        envelope_slope = (-168.0 / CUTOFF) * t5 * (1.0 - t) * (1.0 - t)
        shape_slope = scale * inv * (envelope_slope - envelope * inv)
    for b in range(1, NB + 1):
        value = sines[b] * shape
        for half in range(value.shape[0] // 8):
            basis[half, 8 * b - 8 : 8 * b, :] = value[8 * half : 8 * half + 8]
        if basis_slope is not None:
            basis_slope[8 * b - 8 : 8 * b, :] = (
                (b * math.pi / CUTOFF) * cosines[b] * shape + sines[b] * shape_slope
            )
    return inv, ux, uy, uz


CHARGE_SCRATCH = [
    pltpu.VMEM((136, EXT), f32),
    pltpu.VMEM((288, EXT), bf16),
    pltpu.VMEM((16, ATOM), jnp.int32),
    pltpu.VMEM((2, 8 * NB, ATOM), f32),
    pltpu.VMEM((8, 16, ATOM), f32),
    pltpu.VMEM((K, 3 * C, ATOM), f32),
    pltpu.VMEM((K, C, ATOM), f32),
    pltpu.SemaphoreType.DMA((1,)),
]


def charges_kernel(
    left, own, right, low, high, codes, up_wide, in_wide, out_wide, columns, waves_z,
    spread, charge_out, rel, places_out, along, kept,
    table, split, target_ref, basis, harm, radial, up, sems,
):
    own_pos = own[C : C + 8, :]
    weights_x, _ = spline_rows(own_pos[0:1], PLANE0, 8, False)
    weights_y, _ = spline_rows(own_pos[1:2], ROW0, ROW_PAD, False)

    table[:, 0:128] = left[...]
    table[:, 128:384] = own[...]
    table[:, 384:512] = right[...]
    table[:, 512:576] = low[...]
    table[:, 576:640] = high[...]

    mapped = layered(up_wide, table[0:C, :])
    m_high, m_low = halves(mapped)
    split[0:C, :] = m_high.astype(bf16)
    split[C : 2 * C, :] = m_low.astype(bf16)

    lane = lax.broadcasted_iota(jnp.int32, (8, EXT), 1)
    part = lax.broadcasted_iota(jnp.int32, (8, EXT), 0)
    plane = jnp.where(lane < 512, lane >> 7, (lane >> 4) & 3)
    shift_x = jnp.where(plane == 0, -2.0, jnp.where(plane == 3, 2.0, 0.0))
    shift_y = jnp.where(lane >= 576, 16.0, jnp.where(lane >= 512, -16.0, 0.0))
    places = table[C : C + 8, :] + jnp.where(
        part == 0, shift_x, jnp.where(part == 1, shift_y, 0.0)
    )
    places_out[...] = places
    p_high, p_rest = halves(places)
    p_mid, p_low = halves(p_rest)
    split[2 * C : 2 * C + 32, :] = jnp.concatenate(
        [p_high, p_mid, p_low, jnp.zeros_like(p_low)], axis=0
    ).astype(bf16)

    padded = jnp.concatenate(
        [codes[0:HALF, :], codes[0:2, :], codes[HALF:K, :], codes[0:2, :]], axis=0
    )
    target, wrap = edge_targets(padded)
    target_ref[...] = target
    for k in range(K):
        found = dot(split[...], one_hot(target_ref, slot(k), EXT))
        up[k] = found[0:C] + found[C : 2 * C]
        place = found[256:264] + found[264:272] + found[272:280]
        for c in range(3):
            rel[c, slot(k) : slot(k) + 1, :] = place[c : c + 1]

    keep_up = pltpu.make_async_copy(up, kept, sems.at[0])
    keep_up.start()

    rel_x = rel[0] - own_pos[0:1]
    rel_y = rel[1] - own_pos[1:2]
    rel_z = rel[2] - own_pos[2:3] + wrap.astype(f32) * float(NZ)
    spare = (lax.broadcasted_iota(jnp.int32, (16, ATOM), 0) & 7) >= HALF
    rel_x, rel_y, rel_z = (jnp.where(spare, 1.0, x) for x in (rel_x, rel_y, rel_z))
    rel[0], rel[1], rel[2] = rel_x, rel_y, rel_z
    geometry(rel_x, rel_y, rel_z, harm, basis, None)

    for half in range(2):
        before = layered(in_wide, basis[half])
        hidden = before * jax.nn.sigmoid(before)
        for k in range(HALF):
            radial[HALF * half + k] = layered(out_wide, hidden[RH * k : RH * k + RH])

    charge = []
    site = jnp.zeros((8, 128), f32)
    for half in range(2):
        lanes = slice(128 * half, 128 * half + 128)

        def accumulate(step, carry):
            c0 = pl.multiple_of(step * 8, 8)
            block = pl.ds(c0, 8)
            total = [jnp.zeros((8, 128), f32) for _ in range(9)]
            for k in range(K):
                u = up[k, block, lanes]
                total[0] += radial[k, block, lanes] * u
                first = radial[k, pl.ds(c0 + C, 8), lanes] * u
                second = radial[k, pl.ds(c0 + 2 * C, 8), lanes] * u
                for m in range(8):
                    total[1 + m] += (
                        first if m < 3 else second
                    ) * harm[m, slot(k) : slot(k) + 1, lanes]
            for m in range(8):
                along[m, block, lanes] = total[1 + m] * columns[8 if m < 3 else 9, block, :]
            first = sum(total[m] * total[m] for m in range(1, 4))
            second = sum(total[m] * total[m] for m in range(4, 9))
            feature = own[block, lanes]
            return tuple(
                carry[w]
                + columns[4 * w, block, :] * total[0]
                + columns[4 * w + 1, block, :] * first
                + columns[4 * w + 2, block, :] * second
                + columns[4 * w + 3, block, :] * feature
                for w in range(2)
            )

        zero = jnp.zeros((8, 128), f32)
        sites, charges = lax.fori_loop(0, 16, accumulate, (zero, zero))
        site = site + sites
        charge.append(jnp.sum(charges, axis=0, keepdims=True))
    charge = jnp.concatenate(charge, axis=1)
    charge_out[...] = charge

    charged = weights_y * charge
    planes = jnp.concatenate([charged * weights_x[p : p + 1] for p in OWN_PLANES], axis=0)
    top, rest = halves(planes)
    planes = dot_nt(jnp.concatenate([top, rest, top], axis=1).astype(bf16), waves_z[...])
    lane = lax.broadcasted_iota(jnp.int32, (ROW_PAD, 128), 1)
    row = lax.broadcasted_iota(jnp.int32, (ROW_PAD, 128), 0)
    extra = jnp.where(row == SUM_ROW, spread_out(jnp.sum(site), lane), 0.0)
    for g in range(N_GY):
        part = extra
        for i, p in enumerate(OWN_PLANES):
            amount = (16 * (p - g)) % 128
            moved = planes[ROW_PAD * i : ROW_PAD * i + ROW_PAD]
            moved = pltpu.roll(moved, amount, 1) if amount else moved
            part = jnp.where((lane >> 4) == p, moved, part)
        spread[g] = part
    keep_up.wait()


def y_in_kernel(rows, table, out):
    waves = layered(table, rows[...].reshape(N_GY * ROW_PAD, 128))
    out[:, 0, :] = waves[0:64]
    out[:, 1, :] = waves[64:128]


def x_kernel(planes, x_in, x_out, x_gain, x_square, yz, out):
    sides = jnp.concatenate([planes[:, 0, :], planes[:, 1, :]], axis=1)
    site = jnp.sum(planes[:, 0, SUM_LANE : SUM_LANE + 3])
    waves = layered(x_in, sides)
    filtered = []
    energy = site * (1.0 / (N_GX * N_GY))
    for half in range(2):
        total = jnp.zeros((128, 128), f32)
        for i, p in enumerate(OWN_PLANES):
            block = waves[128 * i : 128 * i + 128, 128 * half : 128 * half + 128]
            total = total + pltpu.roll(block, (128 - 16 * p) % 128, 1)
        square = x_square[...] + yz[0, 2 * half + 1 : 2 * half + 2, :]
        anchor = square == 0.0
        kernel = jnp.where(
            anchor,
            0.0,
            x_gain[...] * yz[0, 2 * half : 2 * half + 1, :] / jnp.where(anchor, 1.0, square),
        )
        shaped = kernel * total
        energy = energy + 0.5 * jnp.sum(shaped * total)
        filtered.append(shaped)
    back = layered(x_out, jnp.concatenate(filtered, axis=1))
    lane = lax.broadcasted_iota(jnp.int32, (64, 128), 1)
    for half in range(2):
        total = spread_out(energy, lane) if half == 0 else jnp.zeros((64, 128), f32)
        for p in range(PLANES):
            block = back[64 * p : 64 * p + 64, 128 * half : 128 * half + 128]
            moved = pltpu.roll(block, 16 * p, 1) if p else block
            total = total + moved
        out[:, half, :] = total


def y_out_kernel(waves, table, out):
    both = jnp.concatenate([waves[:, 0, :], waves[:, 1, :]], axis=0)
    out[...] = layered(table, both).reshape(N_GY, ROW_PAD, 128)


SLOPE_SCRATCH = [
    pltpu.VMEM((1, 8 * NB, ATOM), f32),
    pltpu.VMEM((8 * NB, ATOM), f32),
    pltpu.VMEM((8, 8, ATOM), f32),
    pltpu.VMEM((HALF, 3 * C, ATOM), f32),
    pltpu.VMEM((HALF, 3 * C, ATOM), f32),
    pltpu.VMEM((HALF, 24, ATOM), f32),
    pltpu.VMEM((HALF, C, ATOM), f32),
    pltpu.SemaphoreType.DMA((1,)),
]


def slopes_kernel(
    k0, rel, kept, along, codes, in_wide, out_wide, columns, *refs
):
    scratch = refs[-8:]
    basis, basis_slope, harm, radial, radial_slope, gathered, up, sems = scratch
    before_planes, planes = (refs[0:2], refs[2:4]) if k0 else ((), refs[0:2])
    base = 8 * k0
    for done, plane in zip(before_planes, planes):
        plane[0:base, :] = done[...]
    fetch_up = pltpu.make_async_copy(kept.at[k0 : k0 + HALF], up, sems.at[0])
    fetch_up.start()
    first = slot(k0)
    inv, ux, uy, uz = geometry(
        *(rel[c, first : first + 8, :] for c in range(3)), harm, basis, basis_slope
    )
    before = layered(in_wide, basis[0])
    before_slope = layered(in_wide, basis_slope[...])
    gate = jax.nn.sigmoid(before)
    hidden = before * gate
    hidden_slope = gate * (1.0 + before * (1.0 - gate)) * before_slope
    for k in range(HALF):
        radial[k] = layered(out_wide, hidden[RH * k : RH * k + RH])
        radial_slope[k] = layered(out_wide, hidden_slope[RH * k : RH * k + RH])

    fetch_up.wait()
    for half in range(2):
        spots = slice(128 * half, 128 * half + 128)

        for k in range(HALF):
            total = [jnp.zeros((8, 128), f32) for _ in range(18)]
            shapes = [
                jnp.broadcast_to(harm[m, k : k + 1, spots], (8, 128)) for m in range(8)
            ]
            for block in range(16):
                c0 = 8 * block
                rows = [slice(c0 + C * i, c0 + C * i + 8) for i in range(3)]
                u = up[k, rows[0], spots]
                turn = [along[m, rows[0], spots] for m in range(8)]
                turn_1 = sum(turn[m] * shapes[m] for m in range(3))
                turn_2 = sum(turn[m] * shapes[m] for m in range(3, 8))
                stretch = u * (
                    radial_slope[k, rows[0], spots]
                    + radial_slope[k, rows[1], spots] * turn_1
                    + radial_slope[k, rows[2], spots] * turn_2
                )
                first = radial[k, rows[1], spots] * u
                second = radial[k, rows[2], spots] * u
                for w in range(2):
                    weight = columns[4 * w, rows[0], :]
                    total[9 * w] += weight * stretch
                    first_w = weight * first
                    second_w = weight * second
                    for m in range(8):
                        total[9 * w + 1 + m] += (first_w if m < 3 else second_w) * turn[m]
            sums = [jnp.sum(total[i], axis=0, keepdims=True) for i in range(18)]
            gathered[k, :, spots] = jnp.concatenate(sums + [jnp.zeros((6, 128), f32)], axis=0)

    r3, r5, r15 = math.sqrt(3.0), math.sqrt(5.0), math.sqrt(15.0)
    for w in range(2):
        g = [
            jnp.concatenate(
                [gathered[k, i : i + 1, :] for k in range(HALF)] + [jnp.zeros((2, ATOM), f32)],
                axis=0,
            )
            for i in range(9 * w, 9 * w + 9)
        ]
        vx = r3 * g[1] + r15 * (uy * g[4] + uz * g[7] + ux * g[8])
        vy = r3 * g[2] + r15 * (ux * g[4] + uz * g[5] - uy * g[8])
        vz = r3 * g[3] + r15 * (uy * g[5] + ux * g[7]) + (3.0 * r5) * uz * g[6]
        radial_part = g[0] - (vx * ux + vy * uy + vz * uz) * inv
        for c, (v, along_c) in enumerate(((vx, ux), (vy, uy), (vz, uz))):
            first = base + 8 * (3 * w + c)
            pull = radial_part * along_c + v * inv
            spare = codes[k0 + 2 * c : k0 + 2 * c + 2, :].astype(f32)
            pull = jnp.concatenate([pull[0:HALF], spare if w == 0 else 0.0 * spare], axis=0)
            planes[0][first : first + 8, :] = pull[:, 0:128]
            planes[1][first : first + 8, :] = pull[:, 128:256]


def reach_kernel(places, z_table, out):
    weights, slopes = spline_rows(places[2:3, :], 0, NZ, True)
    both = jnp.concatenate([weights, slopes[:, 128:384]], axis=1)
    out[...] = dot(z_table[...], both, highest)


def final_kernel(
    potential, places, charge, waves, left, lower, upper, right, low, high, forces, energy_out,
    pulls, target_ref,
):
    pulls[:, 0:128] = left[...]
    pulls[:, 128:256] = lower[...]
    pulls[:, 256:384] = upper[...]
    pulls[:, 384:512] = right[...]
    pulls[:, 512:576] = low[...]
    pulls[:, 576:640] = high[...]
    codes = [
        pulls[48 * half + 8 * c + HALF : 48 * half + 8 * c + 8, :]
        for half in range(2)
        for c in range(3)
    ]
    codes = jnp.concatenate(codes, axis=0)
    target_ref[...] = own_targets(codes.astype(jnp.int32))

    mine = slice(128, 384)
    weights_x, slopes_x = spline_rows(places[0:1, :], PLANE0, 8, False)
    weights_y, slopes_y = spline_rows(places[1:2, :], ROW0, ROW_PAD, False)
    lane = lax.broadcasted_iota(jnp.int32, (ROW_PAD, 128), 1)
    energy = jnp.zeros((1, 3), f32)
    for g in range(N_GY):
        energy = energy + potential[g, SUM_ROW : SUM_ROW + 1, SUM_LANE : SUM_LANE + 3]
    energy_out[...] = jnp.sum(energy, axis=1, keepdims=True) * (1.0 / ATOMS_ALL)
    planes = []
    for p in range(PLANES):
        plane = jnp.zeros((ROW_PAD, 128), f32)
        for g in range(N_GY):
            amount = (16 * (g - p)) % 128
            moved = pltpu.roll(potential[g], amount, 1) if amount else potential[g]
            plane = jnp.where((lane >> 4) == g, moved, plane)
        planes.append(plane)
    felt = dot(jnp.concatenate(planes, axis=0), waves[...], highest)
    phi = jnp.zeros((1, EXT), f32)
    slope = [jnp.zeros((1, ATOM), f32)] * 3
    for p in range(PLANES):
        here = felt[ROW_PAD * p : ROW_PAD * p + ROW_PAD, 0:EXT]
        by_y = jnp.sum(here * weights_y, axis=0, keepdims=True)
        phi = phi + by_y * weights_x[p : p + 1]
        slope[0] = slope[0] + by_y[:, mine] * slopes_x[p : p + 1, mine]
        by_y = jnp.sum(here[:, mine] * slopes_y[:, mine], axis=0, keepdims=True)
        slope[1] = slope[1] + by_y * weights_x[p : p + 1, mine]
        here = felt[ROW_PAD * p : ROW_PAD * p + ROW_PAD, EXT:]
        by_y = jnp.sum(here * weights_y[:, mine], axis=0, keepdims=True)
        slope[2] = slope[2] + by_y * weights_x[p : p + 1, mine]

    total = [
        [
            pulls[i + 8 * c : i + 8 * c + 8, :] + phi * pulls[i + 24 + 8 * c : i + 32 + 8 * c, :]
            for c in range(3)
        ]
        for i in (0, 48)
    ]
    table = jnp.zeros((16, ATOM), f32)
    for k in range(K):
        rows = jnp.concatenate(
            [total[k // HALF][c][k % HALF : k % HALF + 1, :] for c in range(3)]
            + [jnp.zeros((5, EXT), f32)],
            axis=0,
        )
        top, rest = halves(rows)
        both = jnp.concatenate([top, rest], axis=0).astype(bf16)
        table = table + dot_nt(both, one_hot(target_ref, k, ATOM))
    for c in range(3):
        forces[c : c + 1, :] = (
            jnp.sum(total[0][c][0:HALF, mine] + total[1][c][0:HALF, mine], axis=0, keepdims=True)
            - table[c : c + 1]
            - table[8 + c : 9 + c]
            - charge[...] * slope[c]
        )


def call(kernel, outs, scratch, flops, *args, far_in=(), far_out=(), mib=8):
    args = [
        pltpu.with_memory_space_constraint(x, pltpu.HBM) if i in far_in else x
        for i, x in enumerate(args)
    ]
    near, far = pl.BlockSpec(memory_space=pltpu.VMEM), pl.BlockSpec(memory_space=pltpu.HBM)
    out_specs = near
    if isinstance(outs, tuple):
        out_specs = tuple(far if i in far_out else near for i in range(len(outs)))
    return pl.pallas_call(
        kernel,
        out_shape=outs,
        in_specs=[far if i in far_in else near for i in range(len(args))],
        out_specs=out_specs,
        scratch_shapes=scratch,
        compiler_params=pltpu.CompilerParams(vmem_limit_bytes=mib * 1024 * 1024),
        cost_estimate=pl.CostEstimate(flops=flops, bytes_accessed=2000000, transcendentals=0),
    )(*args)


def passed_along(array, axis, by):
    devices = lax.axis_size(axis)
    return lax.ppermute(array, axis, [(i, (i + by) % devices) for i in range(devices)])


def plane_ghosts(lower, upper):
    return passed_along(upper, "gx", 1), passed_along(lower, "gx", -1)


def row_ghosts(*planes):
    low = passed_along(jnp.concatenate([x[:, 112:] for x in planes], axis=1), "gy", 1)
    high = passed_along(jnp.concatenate([x[:, :16] for x in planes], axis=1), "gy", -1)
    return low, high


def struct(*shape, dtype=f32):
    return jax.ShapeDtypeStruct(shape, dtype)


def shards(
    positions, features, neighbours, up_weight, radial_in, radial_out, coupling, mix_weight,
    readout, charge_weight,
):
    table = {name: jnp.asarray(value) for name, value in TABLES.items()}
    own = jnp.concatenate([features, positions, jnp.zeros((5, ATOM), f32)], axis=0)
    lower, upper = own[:, 0:128], own[:, 128:256]
    left, right = plane_ghosts(lower, upper)
    low, high = row_ghosts(left, lower, upper, right)
    waves_z, columns, up_wide, in_wide, out_wide = call(
        prepare_kernel,
        (
            struct(NZ, 3 * ATOM, dtype=bf16),
            struct(10, C, 128),
            struct(C, 3 * C, dtype=bf16),
            struct(HALF * RH, 24 * NB, dtype=bf16),
            struct(3 * C, 3 * RH, dtype=bf16),
        ),
        [pltpu.VMEM((8, C), f32)],
        10**8,
        own,
        coupling,
        mix_weight,
        readout.reshape(1, C),
        charge_weight.reshape(1, C),
        up_weight,
        radial_in.T,
        radial_out.T,
        table["z"],
    )
    device = lax.axis_index("gx") * N_GY + lax.axis_index("gy")
    yz = lax.dynamic_slice(table["yz"], (device, 0, 0), (1, 4, 128))

    spread, charge, rel, places, along, kept = call(
        charges_kernel,
        (
            struct(N_GY, ROW_PAD, 128),
            struct(1, ATOM),
            struct(3, 16, ATOM),
            struct(8, EXT),
            struct(8, C, ATOM),
            pltpu.HBM((K, C, ATOM), f32),
        ),
        CHARGE_SCRATCH,
        10**9,
        left,
        own,
        right,
        low,
        high,
        neighbours,
        up_wide,
        in_wide,
        out_wide,
        columns,
        waves_z,
        far_out=(5,),
        mib=28,
    )
    spread, yz = lax.optimization_barrier((spread, yz))

    def pulls_of(k0, kept, *before):
        return call(
            functools.partial(slopes_kernel, k0),
            (struct(8 * k0 + 48, 128),) * 2,
            SLOPE_SCRATCH,
            2 * 10**9,
            rel,
            kept,
            along,
            neighbours,
            in_wide,
            out_wide,
            columns,
            *before,
            far_in=(1,),
            mib=28,
        )

    rows = lax.all_to_all(spread, "gy", split_axis=0, concat_axis=0, tiled=True)
    pulls = pulls_of(0, kept)
    rows, *pulls = lax.optimization_barrier((rows, *pulls))
    waves = call(y_in_kernel, struct(N_GX, 2, 128), [], 10**7, rows, table["y_in"])
    waves, kept = lax.optimization_barrier((waves, kept))
    planes = lax.all_to_all(waves, "gx", split_axis=0, concat_axis=0, tiled=True)
    lower, upper = pulls_of(HALF, kept, *pulls)
    planes, _ = lax.optimization_barrier((planes, lower))
    waves = call(
        x_kernel,
        struct(N_GX, 2, 128),
        [],
        10**7,
        planes,
        table["x_in"],
        table["x_out"],
        table["x_gain"],
        table["x_square"],
        yz,
    )
    reach = call(reach_kernel, struct(NZ, EXT + ATOM), [], 10**8, places, table["z"])
    waves = lax.all_to_all(waves, "gx", split_axis=0, concat_axis=0, tiled=True)
    left, right = plane_ghosts(lower, upper)
    waves, left, right = lax.optimization_barrier((waves, left, right))
    low, high = row_ghosts(left, lower, upper, right)
    rows = call(y_out_kernel, struct(N_GY, ROW_PAD, 128), [], 10**7, waves, table["y_out"])
    potential = lax.all_to_all(rows, "gy", split_axis=0, concat_axis=0, tiled=True)
    forces, energy = call(
        final_kernel,
        (struct(3, ATOM), struct(1, 1)),
        [pltpu.VMEM((96, EXT), f32), pltpu.VMEM((K, EXT), jnp.int32)],
        10**9,
        potential,
        places,
        charge,
        reach,
        left,
        lower,
        upper,
        right,
        low,
        high,
    )
    return (forces, energy.reshape(()))


def solution(mesh):
    placed = (P(None, ("gx", "gy")),) * 3 + (P(),) * 7
    return jax.shard_map(
        shards, mesh=mesh, in_specs=placed, out_specs=(P(None, ("gx", "gy")), P()), check_vma=False
    )
```

```python
import functools
import math

import jax
import jax.numpy as jnp
import ml_dtypes
import numpy as np
from jax import lax
from jax.experimental import pallas as pl
from jax.experimental.pallas import tpu as pltpu
from jax.sharding import PartitionSpec as P

NZ = 128
N_GX = 64
N_GY = 8
K = 12
HALF = K // 2
C = 128
RH = 64
NB = 8
ATOMS_ALL = 131072
ATOM = 256
EXT = 640
CUTOFF = 20.0
BETA = 0.5

PLANE0 = -2
PLANES = 7
OWN_PLANES = range(1, 6)
ROW0 = -3
ROWS = 23
ROW_PAD = 24
SUM_ROW = 23
SUM_LANE = 16 * PLANES

highest = lax.Precision.HIGHEST
f32 = jnp.float32
bf16 = jnp.bfloat16


def real_basis(n):
    cell = np.arange(n)
    rows = [np.full(n, 1.0 / math.sqrt(n))]
    freq = [0]
    for m in range(1, n // 2):
        angle = 2.0 * math.pi / n * (m * cell % n)
        rows += [math.sqrt(2.0 / n) * np.cos(angle), math.sqrt(2.0 / n) * np.sin(angle)]
        freq += [m, m]
    rows.append(np.where(cell % 2 == 0, 1.0, -1.0) / math.sqrt(n))
    freq.append(n // 2)
    return np.stack(rows), np.array(freq)


def tables():
    basis, freq = real_basis(NZ)
    wave = 2.0 * math.pi / NZ * freq
    square = wave * wave
    gain = np.exp(-square / (4.0 * BETA**2)) * (6.0 / (4.0 + 2.0 * np.cos(wave))) ** 2

    plane = (2 * np.arange(N_GX)[None, :] + PLANE0 + np.arange(PLANES)[:, None]) % NZ
    x_in = np.concatenate([basis[:, plane[p]] for p in OWN_PLANES], axis=0)
    x_out = np.concatenate([basis[:, plane[p]].T for p in range(PLANES)], axis=0)

    y_in = np.zeros((NZ, N_GY * ROW_PAD))
    for j in range(N_GY):
        for r in range(ROWS):
            y_in[:, j * ROW_PAD + r] = basis[:, (16 * j + ROW0 + r) % NZ]
        y_in[:, j * ROW_PAD + SUM_ROW] = 1.0

    x_side = np.zeros((NZ, NZ, 2))
    x_side[:, :, 0] = 4.0 * math.pi * gain[:, None]
    x_side[:, :, 1] = square[:, None]

    yz = np.zeros((N_GX * N_GY, 4, 128))
    for i in range(N_GX):
        for j in range(N_GY):
            z = slice(16 * j, 16 * j + 16)
            for half in range(2):
                y = i + 64 * half
                yz[i * N_GY + j, 2 * half, :16] = gain[y] * gain[z]
                yz[i * N_GY + j, 2 * half + 1, :16] = square[y] + square[z]
    as32 = lambda a: np.ascontiguousarray(a, dtype=np.float32)

    def split(a):
        high = as32(a).astype(ml_dtypes.bfloat16)
        low = (as32(a) - high.astype(np.float32)).astype(ml_dtypes.bfloat16)
        return np.concatenate([high, high, low], axis=1)

    return {
        "z": as32(basis),
        "y_in": split(y_in),
        "y_out": split(y_in.T),
        "x_in": split(x_in),
        "x_out": split(x_out),
        "x_gain": as32(x_side[:, :, 0]),
        "x_square": as32(x_side[:, :, 1]),
        "yz": as32(yz),
    }


TABLES = tables()


def dot(a, b, precision=None):
    return jnp.dot(a, b, precision=precision, preferred_element_type=f32)


def dot_nt(a, b, precision=None):
    return lax.dot_general(
        a, b, (((1,), (1,)), ((), ())), precision=precision, preferred_element_type=f32
    )


def halves(x):
    high = x.astype(bf16).astype(f32)
    return high, x - high


def layered(wide, x):
    high, low = halves(x)
    return dot(wide[...], jnp.concatenate([high, low, high], axis=0).astype(bf16))


def spread_out(value, lane):
    high, rest = halves(jnp.full(lane.shape, value, f32))
    mid, low = halves(rest)
    return jnp.where(
        lane == SUM_LANE,
        high,
        jnp.where(lane == SUM_LANE + 1, mid, jnp.where(lane == SUM_LANE + 2, low, 0.0)),
    )


def spline(f):
    g = 1.0 - f
    f2 = f * f
    f3 = f2 * f
    weights = [
        g * g * g / 6.0,
        (3.0 * f3 - 6.0 * f2 + 4.0) / 6.0,
        (-3.0 * f3 + 3.0 * f2 + 3.0 * f + 1.0) / 6.0,
        f3 / 6.0,
    ]
    slopes = [-0.5 * g * g, 1.5 * f2 - 2.0 * f, -1.5 * f2 + f + 0.5, 0.5 * f2]
    return weights, slopes


def spline_rows(u, first, rows, periodic):
    floor = jnp.floor(u)
    base = floor.astype(jnp.int32)
    weights, slopes = spline(u - floor)
    cell = lax.broadcasted_iota(jnp.int32, (rows, u.shape[1]), 0) + first
    table = jnp.zeros((rows, u.shape[1]), f32)
    slope_table = jnp.zeros((rows, u.shape[1]), f32)
    for step in range(4):
        target = base + (step - 1)
        if periodic:
            target = target & (rows - 1)
        hit = cell == target
        table = jnp.where(hit, weights[step], table)
        slope_table = jnp.where(hit, slopes[step], slope_table)
    return table, slope_table


def offsets(codes):
    e = codes + (codes >= 13).astype(jnp.int32)
    nine = (e >= 9).astype(jnp.int32) + (e >= 18).astype(jnp.int32)
    rest = e - 9 * nine
    three = (rest >= 3).astype(jnp.int32) + (rest >= 6).astype(jnp.int32)
    return nine, three, rest - 3 * three - 1


def own_targets(codes):
    nine, three, step_z = offsets(codes)
    n = lax.broadcasted_iota(jnp.int32, codes.shape, 1)
    inner = n < 512
    plane = jnp.where(inner, n >> 7, (n >> 4) & 3) + nine - 2
    row = jnp.where(inner, (n >> 4) & 7, jnp.where(n < 576, -1, 8)) + three - 1
    z = ((n & 15) + step_z) & 15
    here = (plane >= 0) & (plane <= 1) & (row >= 0) & (row <= 7)
    return jnp.where(here, plane * 128 + row * 16 + z, -1)


def edge_targets(codes):
    nine, three, step_z = offsets(codes)
    n = lax.broadcasted_iota(jnp.int32, codes.shape, 1)
    plane = (n >> 7) + nine
    row = ((n >> 4) & 7) + three - 1
    z = (n & 15) + step_z
    wrap = (z >= 16).astype(jnp.int32) - (z < 0).astype(jnp.int32)
    z = z - 16 * wrap
    target = jnp.where(
        row < 0,
        512 + plane * 16 + z,
        jnp.where(row > 7, 576 + plane * 16 + z, plane * 128 + row * 16 + z),
    )
    return target, wrap


def one_hot(target_ref, k, columns):
    lanes = target_ref.shape[1]
    row = jnp.broadcast_to(target_ref[k : k + 1, :], (columns, lanes))
    column = lax.broadcasted_iota(jnp.int32, (columns, lanes), 0)
    return jnp.where(column == row, 1.0, 0.0).astype(bf16)


def beside(x):
    high, low = halves(x)
    return jnp.concatenate([high, high, low], axis=1).astype(bf16)


def prepare_kernel(
    own, coupling, mix_weight, readout, charge_weight, up_weight, radial_in, radial_out, z_table,
    waves_out, columns_out, up_wide, in_wide, out_wide, rows,
):
    weights_z, _ = spline_rows(own[C + 2 : C + 3, :], 0, NZ, True)
    waves_out[...] = beside(dot(z_table[...], weights_z, highest))

    rows[...] = jnp.zeros_like(rows)
    rows[0:1, :] = readout[...]
    rows[1:2, :] = charge_weight[...]
    mixed = dot(rows[...], mix_weight[...], highest) * (1.0 / K)
    for w, direct in enumerate((readout, charge_weight)):
        row = mixed[w : w + 1]
        rows[4 * w : 4 * w + 1, :] = row
        rows[4 * w + 1 : 4 * w + 2, :] = row * coupling[0:1, :] * (1.0 / K)
        rows[4 * w + 2 : 4 * w + 3, :] = row * coupling[1:2, :] * (1.0 / K)
        rows[4 * w + 3 : 4 * w + 4, :] = direct[...]
    standing = rows[...].T
    for i in range(8):
        columns_out[i] = jnp.broadcast_to(standing[:, i : i + 1], (C, 128))
    rows[0:2, :] = coupling[...] * (2.0 / K)
    standing = rows[...].T
    for i in range(2):
        columns_out[8 + i] = jnp.broadcast_to(standing[:, i : i + 1], (C, 128))

    up_wide[...] = beside(up_weight[...])
    out_wide[...] = beside(radial_out[...].T)
    inner = radial_in[...].T
    column = lax.broadcasted_iota(jnp.int32, (NB, 8 * NB), 1)
    wave = lax.broadcasted_iota(jnp.int32, (NB, 8 * NB), 0)
    picks = [jnp.where(column == 8 * wave + k, 1.0, 0.0) for k in range(HALF)]
    in_wide[...] = beside(jnp.concatenate([dot(inner, p, highest) for p in picks], axis=0))


def slot(k):
    return 8 * (k // HALF) + k % HALF


def geometry(rel_x, rel_y, rel_z, harm, basis, basis_slope):
    square = rel_x * rel_x + rel_y * rel_y + rel_z * rel_z
    dist = jnp.sqrt(square)
    inv = 1.0 / dist
    ux, uy, uz = rel_x * inv, rel_y * inv, rel_z * inv
    r3, r5, r15 = math.sqrt(3.0), math.sqrt(5.0), math.sqrt(15.0)
    harmonic = [
        r3 * ux,
        r3 * uy,
        r3 * uz,
        r15 * ux * uy,
        r15 * uy * uz,
        0.5 * r5 * (3.0 * uz * uz - 1.0),
        r15 * ux * uz,
        0.5 * r15 * (ux * ux - uy * uy),
    ]
    for m in range(8):
        harm[m] = harmonic[m]

    t = dist * (1.0 / CUTOFF)
    t2 = t * t
    t4 = t2 * t2
    t5 = t4 * t
    t6 = t4 * t2
    envelope = 1.0 - t6 * (28.0 - t * (48.0 - 21.0 * t))
    theta = math.pi * t
    sines, cosines = {1: jnp.sin(theta)}, {1: jnp.cos(theta)}
    for b in range(2, NB + 1):
        i, j = (b + 1) // 2, b // 2
        sines[b] = sines[i] * cosines[j] + cosines[i] * sines[j]
        cosines[b] = cosines[i] * cosines[j] - sines[i] * sines[j]
    scale = math.sqrt(2.0 / CUTOFF)
    shape = scale * envelope * inv
    if basis_slope is not None:
        envelope_slope = (-168.0 / CUTOFF) * t5 * (1.0 - t) * (1.0 - t)
        shape_slope = scale * inv * (envelope_slope - envelope * inv)
    for b in range(1, NB + 1):
        value = sines[b] * shape
        for half in range(value.shape[0] // 8):
            basis[half, 8 * b - 8 : 8 * b, :] = value[8 * half : 8 * half + 8]
        if basis_slope is not None:
            basis_slope[8 * b - 8 : 8 * b, :] = (
                (b * math.pi / CUTOFF) * cosines[b] * shape + sines[b] * shape_slope
            )
    return inv, ux, uy, uz


CHARGE_SCRATCH = [
    pltpu.VMEM((136, EXT), f32),
    pltpu.VMEM((288, EXT), bf16),
    pltpu.VMEM((16, ATOM), jnp.int32),
    pltpu.VMEM((2, 8 * NB, ATOM), f32),
    pltpu.VMEM((8, 16, ATOM), f32),
    pltpu.VMEM((K, 3 * C, ATOM), f32),
    pltpu.VMEM((K, C, ATOM), f32),
    pltpu.SemaphoreType.DMA((4,)),
]


def charges_kernel(
    left, own, right, low, high, codes, up_wide, in_wide, out_wide, columns, waves_z,
    spread, charge_out, rel, places_out, along, kept,
    table, split, target_ref, basis, harm, radial, up, sems,
):
    own_pos = own[C : C + 8, :]
    weights_x, _ = spline_rows(own_pos[0:1], PLANE0, 8, False)
    weights_y, _ = spline_rows(own_pos[1:2], ROW0, ROW_PAD, False)

    table[:, 0:128] = left[...]
    table[:, 128:384] = own[...]
    table[:, 384:512] = right[...]
    table[:, 512:576] = low[...]
    table[:, 576:640] = high[...]

    mapped = layered(up_wide, table[0:C, :])
    m_high, m_low = halves(mapped)
    split[0:C, :] = m_high.astype(bf16)
    split[C : 2 * C, :] = m_low.astype(bf16)

    lane = lax.broadcasted_iota(jnp.int32, (8, EXT), 1)
    part = lax.broadcasted_iota(jnp.int32, (8, EXT), 0)
    plane = jnp.where(lane < 512, lane >> 7, (lane >> 4) & 3)
    shift_x = jnp.where(plane == 0, -2.0, jnp.where(plane == 3, 2.0, 0.0))
    shift_y = jnp.where(lane >= 576, 16.0, jnp.where(lane >= 512, -16.0, 0.0))
    places = table[C : C + 8, :] + jnp.where(
        part == 0, shift_x, jnp.where(part == 1, shift_y, 0.0)
    )
    places_out[...] = places
    p_high, p_rest = halves(places)
    p_mid, p_low = halves(p_rest)
    split[2 * C : 2 * C + 32, :] = jnp.concatenate(
        [p_high, p_mid, p_low, jnp.zeros_like(p_low)], axis=0
    ).astype(bf16)

    padded = jnp.concatenate(
        [codes[0:HALF, :], codes[0:2, :], codes[HALF:K, :], codes[0:2, :]], axis=0
    )
    target, wrap = edge_targets(padded)
    target_ref[...] = target
    keep = []
    for k in range(K):
        found = dot(split[...], one_hot(target_ref, slot(k), EXT))
        up[k] = found[0:C] + found[C : 2 * C]
        place = found[256:264] + found[264:272] + found[272:280]
        for c in range(3):
            rel[c, slot(k) : slot(k) + 1, :] = place[c : c + 1]
        if k % 3 == 2:
            some = slice(k - 2, k + 1)
            keep.append(pltpu.make_async_copy(up.at[some], kept.at[some], sems.at[k // 3]))
            keep[-1].start()

    rel_x = rel[0] - own_pos[0:1]
    rel_y = rel[1] - own_pos[1:2]
    rel_z = rel[2] - own_pos[2:3] + wrap.astype(f32) * float(NZ)
    spare = (lax.broadcasted_iota(jnp.int32, (16, ATOM), 0) & 7) >= HALF
    rel_x, rel_y, rel_z = (jnp.where(spare, 1.0, x) for x in (rel_x, rel_y, rel_z))
    rel[0], rel[1], rel[2] = rel_x, rel_y, rel_z
    geometry(rel_x, rel_y, rel_z, harm, basis, None)

    for half in range(2):
        before = layered(in_wide, basis[half])
        hidden = before * jax.nn.sigmoid(before)
        for k in range(HALF):
            radial[HALF * half + k] = layered(out_wide, hidden[RH * k : RH * k + RH])

    charge = []
    site = jnp.zeros((8, 128), f32)
    for half in range(2):
        lanes = slice(128 * half, 128 * half + 128)

        def accumulate(step, carry):
            c0 = pl.multiple_of(step * 8, 8)
            block = pl.ds(c0, 8)
            total = [jnp.zeros((8, 128), f32) for _ in range(9)]
            for k in range(K):
                u = up[k, block, lanes]
                total[0] += radial[k, block, lanes] * u
                first = radial[k, pl.ds(c0 + C, 8), lanes] * u
                second = radial[k, pl.ds(c0 + 2 * C, 8), lanes] * u
                for m in range(8):
                    total[1 + m] += (
                        first if m < 3 else second
                    ) * harm[m, slot(k) : slot(k) + 1, lanes]
            for m in range(8):
                along[m, block, lanes] = total[1 + m] * columns[8 if m < 3 else 9, block, :]
            first = sum(total[m] * total[m] for m in range(1, 4))
            second = sum(total[m] * total[m] for m in range(4, 9))
            feature = own[block, lanes]
            return tuple(
                carry[w]
                + columns[4 * w, block, :] * total[0]
                + columns[4 * w + 1, block, :] * first
                + columns[4 * w + 2, block, :] * second
                + columns[4 * w + 3, block, :] * feature
                for w in range(2)
            )

        zero = jnp.zeros((8, 128), f32)
        sites, charges = lax.fori_loop(0, 16, accumulate, (zero, zero), unroll=16)
        site = site + sites
        charge.append(jnp.sum(charges, axis=0, keepdims=True))
    charge = jnp.concatenate(charge, axis=1)
    charge_out[...] = charge

    charged = weights_y * charge
    planes = jnp.concatenate([charged * weights_x[p : p + 1] for p in OWN_PLANES], axis=0)
    top, rest = halves(planes)
    planes = dot_nt(jnp.concatenate([top, rest, top], axis=1).astype(bf16), waves_z[...])
    lane = lax.broadcasted_iota(jnp.int32, (ROW_PAD, 128), 1)
    row = lax.broadcasted_iota(jnp.int32, (ROW_PAD, 128), 0)
    extra = jnp.where(row == SUM_ROW, spread_out(jnp.sum(site), lane), 0.0)
    for g in range(N_GY):
        part = extra
        for i, p in enumerate(OWN_PLANES):
            amount = (16 * (p - g)) % 128
            moved = planes[ROW_PAD * i : ROW_PAD * i + ROW_PAD]
            moved = pltpu.roll(moved, amount, 1) if amount else moved
            part = jnp.where((lane >> 4) == p, moved, part)
        spread[g] = part
    for copy in keep:
        copy.wait()


def y_in_kernel(rows, table, out):
    waves = layered(table, rows[...].reshape(N_GY * ROW_PAD, 128))
    out[:, 0, :] = waves[0:64]
    out[:, 1, :] = waves[64:128]


def x_kernel(planes, x_in, x_out, x_gain, x_square, yz, out):
    sides = jnp.concatenate([planes[:, 0, :], planes[:, 1, :]], axis=1)
    site = jnp.sum(planes[:, 0, SUM_LANE : SUM_LANE + 3])
    waves = layered(x_in, sides)
    filtered = []
    energy = site * (1.0 / (N_GX * N_GY))
    for half in range(2):
        total = jnp.zeros((128, 128), f32)
        for i, p in enumerate(OWN_PLANES):
            block = waves[128 * i : 128 * i + 128, 128 * half : 128 * half + 128]
            total = total + pltpu.roll(block, (128 - 16 * p) % 128, 1)
        square = x_square[...] + yz[0, 2 * half + 1 : 2 * half + 2, :]
        anchor = square == 0.0
        kernel = jnp.where(
            anchor,
            0.0,
            x_gain[...] * yz[0, 2 * half : 2 * half + 1, :] / jnp.where(anchor, 1.0, square),
        )
        shaped = kernel * total
        energy = energy + 0.5 * jnp.sum(shaped * total)
        filtered.append(shaped)
    back = layered(x_out, jnp.concatenate(filtered, axis=1))
    lane = lax.broadcasted_iota(jnp.int32, (64, 128), 1)
    for half in range(2):
        total = spread_out(energy, lane) if half == 0 else jnp.zeros((64, 128), f32)
        for p in range(PLANES):
            block = back[64 * p : 64 * p + 64, 128 * half : 128 * half + 128]
            moved = pltpu.roll(block, 16 * p, 1) if p else block
            total = total + moved
        out[:, half, :] = total


def y_out_kernel(waves, table, out):
    both = jnp.concatenate([waves[:, 0, :], waves[:, 1, :]], axis=0)
    out[...] = layered(table, both).reshape(N_GY, ROW_PAD, 128)


SLOPE_SCRATCH = [
    pltpu.VMEM((1, 8 * NB, ATOM), f32),
    pltpu.VMEM((8 * NB, ATOM), f32),
    pltpu.VMEM((8, 8, ATOM), f32),
    pltpu.VMEM((HALF, 3 * C, ATOM), f32),
    pltpu.VMEM((HALF, 3 * C, ATOM), f32),
    pltpu.VMEM((HALF, 24, ATOM), f32),
    pltpu.VMEM((HALF, C, ATOM), f32),
    pltpu.SemaphoreType.DMA((3,)),
]


def slopes_kernel(
    k0, rel, kept, along, codes, in_wide, out_wide, columns, *refs
):
    scratch = refs[-8:]
    basis, basis_slope, harm, radial, radial_slope, gathered, up, sems = scratch
    before_planes, planes = (refs[0:2], refs[2:4]) if k0 else ((), refs[0:2])
    base = 8 * k0
    for done, plane in zip(before_planes, planes):
        plane[0:base, :] = done[...]
    fetch = [
        pltpu.make_async_copy(kept.at[k0 + k : k0 + k + 2], up.at[k : k + 2], sems.at[k // 2])
        for k in range(0, HALF, 2)
    ]
    for copy in fetch:
        copy.start()
    first = slot(k0)
    inv, ux, uy, uz = geometry(
        *(rel[c, first : first + 8, :] for c in range(3)), harm, basis, basis_slope
    )
    before = layered(in_wide, basis[0])
    before_slope = layered(in_wide, basis_slope[...])
    gate = jax.nn.sigmoid(before)
    hidden = before * gate
    hidden_slope = gate * (1.0 + before * (1.0 - gate)) * before_slope
    for k in range(HALF):
        radial[k] = layered(out_wide, hidden[RH * k : RH * k + RH])
        radial_slope[k] = layered(out_wide, hidden_slope[RH * k : RH * k + RH])

    for copy in fetch:
        copy.wait()
    for half in range(2):
        spots = slice(128 * half, 128 * half + 128)

        for k in range(HALF):
            total = [jnp.zeros((8, 128), f32) for _ in range(18)]
            shapes = [
                jnp.broadcast_to(harm[m, k : k + 1, spots], (8, 128)) for m in range(8)
            ]
            for block in range(16):
                c0 = 8 * block
                rows = [slice(c0 + C * i, c0 + C * i + 8) for i in range(3)]
                u = up[k, rows[0], spots]
                turn = [along[m, rows[0], spots] for m in range(8)]
                turn_1 = sum(turn[m] * shapes[m] for m in range(3))
                turn_2 = sum(turn[m] * shapes[m] for m in range(3, 8))
                stretch = u * (
                    radial_slope[k, rows[0], spots]
                    + radial_slope[k, rows[1], spots] * turn_1
                    + radial_slope[k, rows[2], spots] * turn_2
                )
                first = radial[k, rows[1], spots] * u
                second = radial[k, rows[2], spots] * u
                for w in range(2):
                    weight = columns[4 * w, rows[0], :]
                    total[9 * w] += weight * stretch
                    first_w = weight * first
                    second_w = weight * second
                    for m in range(8):
                        total[9 * w + 1 + m] += (first_w if m < 3 else second_w) * turn[m]
            sums = [jnp.sum(total[i], axis=0, keepdims=True) for i in range(18)]
            gathered[k, :, spots] = jnp.concatenate(sums + [jnp.zeros((6, 128), f32)], axis=0)

    r3, r5, r15 = math.sqrt(3.0), math.sqrt(5.0), math.sqrt(15.0)
    for w in range(2):
        g = [
            jnp.concatenate(
                [gathered[k, i : i + 1, :] for k in range(HALF)] + [jnp.zeros((2, ATOM), f32)],
                axis=0,
            )
            for i in range(9 * w, 9 * w + 9)
        ]
        vx = r3 * g[1] + r15 * (uy * g[4] + uz * g[7] + ux * g[8])
        vy = r3 * g[2] + r15 * (ux * g[4] + uz * g[5] - uy * g[8])
        vz = r3 * g[3] + r15 * (uy * g[5] + ux * g[7]) + (3.0 * r5) * uz * g[6]
        radial_part = g[0] - (vx * ux + vy * uy + vz * uz) * inv
        for c, (v, along_c) in enumerate(((vx, ux), (vy, uy), (vz, uz))):
            first = base + 8 * (3 * w + c)
            pull = radial_part * along_c + v * inv
            spare = codes[k0 + 2 * c : k0 + 2 * c + 2, :].astype(f32)
            pull = jnp.concatenate([pull[0:HALF], spare if w == 0 else 0.0 * spare], axis=0)
            planes[0][first : first + 8, :] = pull[:, 0:128]
            planes[1][first : first + 8, :] = pull[:, 128:256]


def reach_kernel(places, z_table, out):
    weights, slopes = spline_rows(places[2:3, :], 0, NZ, True)
    both = jnp.concatenate([weights, slopes[:, 128:384]], axis=1)
    high, low = halves(dot(z_table[...], both, highest))
    out[...] = jnp.concatenate([high, low, high], axis=0).astype(bf16)


def final_kernel(
    potential, places, charge, waves, left, lower, upper, right, low, high, forces, energy_out,
    pulls, target_ref,
):
    pulls[:, 0:128] = left[...]
    pulls[:, 128:256] = lower[...]
    pulls[:, 256:384] = upper[...]
    pulls[:, 384:512] = right[...]
    pulls[:, 512:576] = low[...]
    pulls[:, 576:640] = high[...]
    codes = [
        pulls[48 * half + 8 * c + HALF : 48 * half + 8 * c + 8, :]
        for half in range(2)
        for c in range(3)
    ]
    codes = jnp.concatenate(codes, axis=0)
    target_ref[...] = own_targets(codes.astype(jnp.int32))

    mine = slice(128, 384)
    weights_x, slopes_x = spline_rows(places[0:1, :], PLANE0, 8, False)
    weights_y, slopes_y = spline_rows(places[1:2, :], ROW0, ROW_PAD, False)
    lane = lax.broadcasted_iota(jnp.int32, (ROW_PAD, 128), 1)
    energy = jnp.zeros((1, 3), f32)
    for g in range(N_GY):
        energy = energy + potential[g, SUM_ROW : SUM_ROW + 1, SUM_LANE : SUM_LANE + 3]
    energy_out[...] = jnp.sum(energy, axis=1, keepdims=True) * (1.0 / ATOMS_ALL)
    planes = []
    for p in range(PLANES):
        plane = jnp.zeros((ROW_PAD, 128), f32)
        for g in range(N_GY):
            amount = (16 * (g - p)) % 128
            moved = pltpu.roll(potential[g], amount, 1) if amount else potential[g]
            plane = jnp.where((lane >> 4) == g, moved, plane)
        planes.append(plane)
    felt = dot(beside(jnp.concatenate(planes, axis=0)), waves[...])
    phi = jnp.zeros((1, EXT), f32)
    slope = [jnp.zeros((1, ATOM), f32)] * 3
    for p in range(PLANES):
        here = felt[ROW_PAD * p : ROW_PAD * p + ROW_PAD, 0:EXT]
        by_y = jnp.sum(here * weights_y, axis=0, keepdims=True)
        phi = phi + by_y * weights_x[p : p + 1]
        slope[0] = slope[0] + by_y[:, mine] * slopes_x[p : p + 1, mine]
        by_y = jnp.sum(here[:, mine] * slopes_y[:, mine], axis=0, keepdims=True)
        slope[1] = slope[1] + by_y * weights_x[p : p + 1, mine]
        here = felt[ROW_PAD * p : ROW_PAD * p + ROW_PAD, EXT:]
        by_y = jnp.sum(here * weights_y[:, mine], axis=0, keepdims=True)
        slope[2] = slope[2] + by_y * weights_x[p : p + 1, mine]

    total = [
        [
            pulls[i + 8 * c : i + 8 * c + 8, :] + phi * pulls[i + 24 + 8 * c : i + 32 + 8 * c, :]
            for c in range(3)
        ]
        for i in (0, 48)
    ]
    part = lax.broadcasted_iota(jnp.int32, (16, EXT), 0)
    table = jnp.zeros((96, 16), f32)
    for k in range(K):
        rows = jnp.concatenate(
            [total[k // HALF][c][k % HALF : k % HALF + 1, :] for c in range(3)]
            + [jnp.zeros((5, EXT), f32)],
            axis=0,
        )
        target = target_ref[k : k + 1, :]
        here = part == (target >> 4)
        by_row = [
            jnp.where(here, x[c : c + 1, :], 0.0) for x in halves(rows) for c in range(3)
        ]
        by_site = jnp.where(part == (target & 15), 1.0, 0.0).astype(bf16)
        table = table + dot_nt(jnp.concatenate(by_row, axis=0).astype(bf16), by_site)
    table = table[0:48] + table[48:96]
    table = jnp.concatenate([table, jnp.zeros((48, 112), f32)], axis=1)
    for c in range(3):
        ends = []
        for plane in range(2):
            lanes = table[16 * c + 8 * plane : 16 * c + 8 * plane + 1]
            for a in range(1, 8):
                row = 16 * c + 8 * plane + a
                lanes = lanes + pltpu.roll(table[row : row + 1], 16 * a, 1)
            ends.append(lanes)
        forces[c : c + 1, :] = (
            jnp.sum(total[0][c][0:HALF, mine] + total[1][c][0:HALF, mine], axis=0, keepdims=True)
            - jnp.concatenate(ends, axis=1)
            - charge[...] * slope[c]
        )


def call(kernel, outs, scratch, flops, *args, far_in=(), far_out=(), mib=8):
    args = [
        pltpu.with_memory_space_constraint(x, pltpu.HBM) if i in far_in else x
        for i, x in enumerate(args)
    ]
    near, far = pl.BlockSpec(memory_space=pltpu.VMEM), pl.BlockSpec(memory_space=pltpu.HBM)
    out_specs = near
    if isinstance(outs, tuple):
        out_specs = tuple(far if i in far_out else near for i in range(len(outs)))
    return pl.pallas_call(
        kernel,
        out_shape=outs,
        in_specs=[far if i in far_in else near for i in range(len(args))],
        out_specs=out_specs,
        scratch_shapes=scratch,
        compiler_params=pltpu.CompilerParams(vmem_limit_bytes=mib * 1024 * 1024),
        cost_estimate=pl.CostEstimate(flops=flops, bytes_accessed=2000000, transcendentals=0),
    )(*args)


def passed_along(array, axis, by):
    devices = lax.axis_size(axis)
    return lax.ppermute(array, axis, [(i, (i + by) % devices) for i in range(devices)])


def plane_ghosts(lower, upper):
    return passed_along(upper, "gx", 1), passed_along(lower, "gx", -1)


def row_ghosts(*planes):
    low = passed_along(jnp.concatenate([x[:, 112:] for x in planes], axis=1), "gy", 1)
    high = passed_along(jnp.concatenate([x[:, :16] for x in planes], axis=1), "gy", -1)
    return low, high


def struct(*shape, dtype=f32):
    return jax.ShapeDtypeStruct(shape, dtype)


def shards(
    positions, features, neighbours, up_weight, radial_in, radial_out, coupling, mix_weight,
    readout, charge_weight,
):
    table = {name: jnp.asarray(value) for name, value in TABLES.items()}
    own = jnp.concatenate([features, positions, jnp.zeros((5, ATOM), f32)], axis=0)
    lower, upper = own[:, 0:128], own[:, 128:256]
    left, right = plane_ghosts(lower, upper)
    low, high = row_ghosts(left, lower, upper, right)
    waves_z, columns, up_wide, in_wide, out_wide = call(
        prepare_kernel,
        (
            struct(NZ, 3 * ATOM, dtype=bf16),
            struct(10, C, 128),
            struct(C, 3 * C, dtype=bf16),
            struct(HALF * RH, 24 * NB, dtype=bf16),
            struct(3 * C, 3 * RH, dtype=bf16),
        ),
        [pltpu.VMEM((8, C), f32)],
        10**8,
        own,
        coupling,
        mix_weight,
        readout.reshape(1, C),
        charge_weight.reshape(1, C),
        up_weight,
        radial_in.T,
        radial_out.T,
        table["z"],
    )
    device = lax.axis_index("gx") * N_GY + lax.axis_index("gy")
    yz = lax.dynamic_slice(table["yz"], (device, 0, 0), (1, 4, 128))

    spread, charge, rel, places, along, kept = call(
        charges_kernel,
        (
            struct(N_GY, ROW_PAD, 128),
            struct(1, ATOM),
            struct(3, 16, ATOM),
            struct(8, EXT),
            struct(8, C, ATOM),
            pltpu.HBM((K, C, ATOM), f32),
        ),
        CHARGE_SCRATCH,
        10**9,
        left,
        own,
        right,
        low,
        high,
        neighbours,
        up_wide,
        in_wide,
        out_wide,
        columns,
        waves_z,
        far_out=(5,),
        mib=28,
    )
    spread, yz = lax.optimization_barrier((spread, yz))

    def pulls_of(k0, kept, *before):
        return call(
            functools.partial(slopes_kernel, k0),
            (struct(8 * k0 + 48, 128),) * 2,
            SLOPE_SCRATCH,
            2 * 10**9,
            rel,
            kept,
            along,
            neighbours,
            in_wide,
            out_wide,
            columns,
            *before,
            far_in=(1,),
            mib=28,
        )

    rows = lax.all_to_all(spread, "gy", split_axis=0, concat_axis=0, tiled=True)
    pulls = pulls_of(0, kept)
    rows, *pulls = lax.optimization_barrier((rows, *pulls))
    waves = call(y_in_kernel, struct(N_GX, 2, 128), [], 10**7, rows, table["y_in"])
    waves, kept = lax.optimization_barrier((waves, kept))
    planes = lax.all_to_all(waves, "gx", split_axis=0, concat_axis=0, tiled=True)
    lower, upper = pulls_of(HALF, kept, *pulls)
    planes, _ = lax.optimization_barrier((planes, lower))
    waves = call(
        x_kernel,
        struct(N_GX, 2, 128),
        [],
        10**7,
        planes,
        table["x_in"],
        table["x_out"],
        table["x_gain"],
        table["x_square"],
        yz,
    )
    reach = call(reach_kernel, struct(3 * NZ, EXT + ATOM, dtype=bf16), [], 10**8, places, table["z"])
    waves = lax.all_to_all(waves, "gx", split_axis=0, concat_axis=0, tiled=True)
    left, right = plane_ghosts(lower, upper)
    waves, left, right = lax.optimization_barrier((waves, left, right))
    low, high = row_ghosts(left, lower, upper, right)
    rows = call(y_out_kernel, struct(N_GY, ROW_PAD, 128), [], 10**7, waves, table["y_out"])
    potential = lax.all_to_all(rows, "gy", split_axis=0, concat_axis=0, tiled=True)
    forces, energy = call(
        final_kernel,
        (struct(3, ATOM), struct(1, 1)),
        [pltpu.VMEM((96, EXT), f32), pltpu.VMEM((K, EXT), jnp.int32)],
        10**9,
        potential,
        places,
        charge,
        reach,
        left,
        lower,
        upper,
        right,
        low,
        high,
    )
    return (forces, energy.reshape(()))


def solution(mesh):
    placed = (P(None, ("gx", "gy")),) * 3 + (P(),) * 7
    return jax.shard_map(
        shards, mesh=mesh, in_specs=placed, out_specs=(P(None, ("gx", "gy")), P()), check_vma=False
    )
```

```python
import functools
import math

import jax
import jax.numpy as jnp
import ml_dtypes
import numpy as np
from jax import lax
from jax.experimental import pallas as pl
from jax.experimental.pallas import tpu as pltpu
from jax.sharding import PartitionSpec as P

NZ = 128
N_GX = 64
N_GY = 8
K = 12
HALF = K // 2
C = 128
RH = 64
NB = 8
ATOMS_ALL = 131072
ATOM = 256
EXT = 640
CUTOFF = 20.0
BETA = 0.5

PLANE0 = -2
PLANES = 7
OWN_PLANES = range(1, 6)
ROW0 = -3
ROWS = 23
ROW_PAD = 24
SUM_ROW = 23
SUM_LANE = 16 * PLANES

highest = lax.Precision.HIGHEST
f32 = jnp.float32
bf16 = jnp.bfloat16


def real_basis(n):
    cell = np.arange(n)
    rows = [np.full(n, 1.0 / math.sqrt(n))]
    freq = [0]
    for m in range(1, n // 2):
        angle = 2.0 * math.pi / n * (m * cell % n)
        rows += [math.sqrt(2.0 / n) * np.cos(angle), math.sqrt(2.0 / n) * np.sin(angle)]
        freq += [m, m]
    rows.append(np.where(cell % 2 == 0, 1.0, -1.0) / math.sqrt(n))
    freq.append(n // 2)
    return np.stack(rows), np.array(freq)


def tables():
    basis, freq = real_basis(NZ)
    wave = 2.0 * math.pi / NZ * freq
    square = wave * wave
    gain = np.exp(-square / (4.0 * BETA**2)) * (6.0 / (4.0 + 2.0 * np.cos(wave))) ** 2

    plane = (2 * np.arange(N_GX)[None, :] + PLANE0 + np.arange(PLANES)[:, None]) % NZ
    x_in = np.concatenate([basis[:, plane[p]] for p in OWN_PLANES], axis=0)
    x_out = np.concatenate([basis[:, plane[p]].T for p in range(PLANES)], axis=0)

    y_in = np.zeros((NZ, N_GY * ROW_PAD))
    for j in range(N_GY):
        for r in range(ROWS):
            y_in[:, j * ROW_PAD + r] = basis[:, (16 * j + ROW0 + r) % NZ]
        y_in[:, j * ROW_PAD + SUM_ROW] = 1.0

    x_side = np.zeros((NZ, NZ, 2))
    x_side[:, :, 0] = 4.0 * math.pi * gain[:, None]
    x_side[:, :, 1] = square[:, None]

    yz = np.zeros((N_GX * N_GY, 4, 128))
    for i in range(N_GX):
        for j in range(N_GY):
            z = slice(16 * j, 16 * j + 16)
            for half in range(2):
                y = i + 64 * half
                yz[i * N_GY + j, 2 * half, :16] = gain[y] * gain[z]
                yz[i * N_GY + j, 2 * half + 1, :16] = square[y] + square[z]
    as32 = lambda a: np.ascontiguousarray(a, dtype=np.float32)

    def split(a):
        high = as32(a).astype(ml_dtypes.bfloat16)
        low = (as32(a) - high.astype(np.float32)).astype(ml_dtypes.bfloat16)
        return np.concatenate([high, high, low], axis=1)

    return {
        "z": as32(basis),
        "y_in": split(y_in),
        "y_out": split(y_in.T),
        "x_in": split(x_in),
        "x_out": split(x_out),
        "x_gain": as32(x_side[:, :, 0]),
        "x_square": as32(x_side[:, :, 1]),
        "yz": as32(yz),
    }


TABLES = tables()


def dot(a, b, precision=None):
    return jnp.dot(a, b, precision=precision, preferred_element_type=f32)


def dot_nt(a, b, precision=None):
    return lax.dot_general(
        a, b, (((1,), (1,)), ((), ())), precision=precision, preferred_element_type=f32
    )


def halves(x):
    high = x.astype(bf16).astype(f32)
    return high, x - high


def layered(wide, x):
    high, low = halves(x)
    return dot(wide[...], jnp.concatenate([high, low, high], axis=0).astype(bf16))


def spread_out(value, lane):
    high, rest = halves(jnp.full(lane.shape, value, f32))
    mid, low = halves(rest)
    return jnp.where(
        lane == SUM_LANE,
        high,
        jnp.where(lane == SUM_LANE + 1, mid, jnp.where(lane == SUM_LANE + 2, low, 0.0)),
    )


def spline(f):
    g = 1.0 - f
    f2 = f * f
    f3 = f2 * f
    weights = [
        g * g * g / 6.0,
        (3.0 * f3 - 6.0 * f2 + 4.0) / 6.0,
        (-3.0 * f3 + 3.0 * f2 + 3.0 * f + 1.0) / 6.0,
        f3 / 6.0,
    ]
    slopes = [-0.5 * g * g, 1.5 * f2 - 2.0 * f, -1.5 * f2 + f + 0.5, 0.5 * f2]
    return weights, slopes


def spline_rows(u, first, rows, periodic):
    floor = jnp.floor(u)
    base = floor.astype(jnp.int32)
    weights, slopes = spline(u - floor)
    cell = lax.broadcasted_iota(jnp.int32, (rows, u.shape[1]), 0) + first
    table = jnp.zeros((rows, u.shape[1]), f32)
    slope_table = jnp.zeros((rows, u.shape[1]), f32)
    for step in range(4):
        target = base + (step - 1)
        if periodic:
            target = target & (rows - 1)
        hit = cell == target
        table = jnp.where(hit, weights[step], table)
        slope_table = jnp.where(hit, slopes[step], slope_table)
    return table, slope_table


def offsets(codes):
    e = codes + (codes >= 13).astype(jnp.int32)
    nine = (e >= 9).astype(jnp.int32) + (e >= 18).astype(jnp.int32)
    rest = e - 9 * nine
    three = (rest >= 3).astype(jnp.int32) + (rest >= 6).astype(jnp.int32)
    return nine, three, rest - 3 * three - 1


def own_targets(codes):
    nine, three, step_z = offsets(codes)
    n = lax.broadcasted_iota(jnp.int32, codes.shape, 1)
    inner = n < 512
    plane = jnp.where(inner, n >> 7, (n >> 4) & 3) + nine - 2
    row = jnp.where(inner, (n >> 4) & 7, jnp.where(n < 576, -1, 8)) + three - 1
    z = ((n & 15) + step_z) & 15
    here = (plane >= 0) & (plane <= 1) & (row >= 0) & (row <= 7)
    return jnp.where(here, plane * 128 + row * 16 + z, -1)


def edge_targets(codes):
    nine, three, step_z = offsets(codes)
    n = lax.broadcasted_iota(jnp.int32, codes.shape, 1)
    plane = (n >> 7) + nine
    row = ((n >> 4) & 7) + three - 1
    z = (n & 15) + step_z
    wrap = (z >= 16).astype(jnp.int32) - (z < 0).astype(jnp.int32)
    z = z - 16 * wrap
    target = jnp.where(
        row < 0,
        512 + plane * 16 + z,
        jnp.where(row > 7, 576 + plane * 16 + z, plane * 128 + row * 16 + z),
    )
    return target, wrap


def one_hot(target_ref, k, columns):
    lanes = target_ref.shape[1]
    row = jnp.broadcast_to(target_ref[k : k + 1, :], (columns, lanes))
    column = lax.broadcasted_iota(jnp.int32, (columns, lanes), 0)
    return jnp.where(column == row, 1.0, 0.0).astype(bf16)


def beside(x):
    high, low = halves(x)
    return jnp.concatenate([high, high, low], axis=1).astype(bf16)


def prepare_kernel(
    own, coupling, mix_weight, readout, charge_weight, up_weight, radial_in, radial_out, z_table,
    waves_out, columns_out, up_wide, in_wide, out_wide, rows,
):
    weights_z, _ = spline_rows(own[C + 2 : C + 3, :], 0, NZ, True)
    waves_out[...] = beside(dot(z_table[...], weights_z, highest))

    rows[...] = jnp.zeros_like(rows)
    rows[0:1, :] = readout[...]
    rows[1:2, :] = charge_weight[...]
    mixed = dot(rows[...], mix_weight[...], highest) * (1.0 / K)
    for w, direct in enumerate((readout, charge_weight)):
        row = mixed[w : w + 1]
        rows[4 * w : 4 * w + 1, :] = row
        rows[4 * w + 1 : 4 * w + 2, :] = row * coupling[0:1, :] * (1.0 / K)
        rows[4 * w + 2 : 4 * w + 3, :] = row * coupling[1:2, :] * (1.0 / K)
        rows[4 * w + 3 : 4 * w + 4, :] = direct[...]
    standing = rows[...].T
    for i in range(8):
        columns_out[i] = jnp.broadcast_to(standing[:, i : i + 1], (C, 128))
    rows[0:2, :] = coupling[...] * (2.0 / K)
    standing = rows[...].T
    for i in range(2):
        columns_out[8 + i] = jnp.broadcast_to(standing[:, i : i + 1], (C, 128))

    up_wide[...] = beside(up_weight[...])
    out_wide[...] = beside(radial_out[...].T)
    inner = radial_in[...].T
    column = lax.broadcasted_iota(jnp.int32, (NB, 8 * NB), 1)
    wave = lax.broadcasted_iota(jnp.int32, (NB, 8 * NB), 0)
    picks = [jnp.where(column == 8 * wave + k, 1.0, 0.0) for k in range(HALF)]
    in_wide[...] = beside(jnp.concatenate([dot(inner, p, highest) for p in picks], axis=0))


def slot(k):
    return 8 * (k // HALF) + k % HALF


def geometry(rel_x, rel_y, rel_z, harm, basis, basis_slope):
    square = rel_x * rel_x + rel_y * rel_y + rel_z * rel_z
    dist = jnp.sqrt(square)
    inv = 1.0 / dist
    ux, uy, uz = rel_x * inv, rel_y * inv, rel_z * inv
    r3, r5, r15 = math.sqrt(3.0), math.sqrt(5.0), math.sqrt(15.0)
    harmonic = [
        r3 * ux,
        r3 * uy,
        r3 * uz,
        r15 * ux * uy,
        r15 * uy * uz,
        0.5 * r5 * (3.0 * uz * uz - 1.0),
        r15 * ux * uz,
        0.5 * r15 * (ux * ux - uy * uy),
    ]
    for m in range(8):
        harm[m] = harmonic[m]

    t = dist * (1.0 / CUTOFF)
    t2 = t * t
    t4 = t2 * t2
    t5 = t4 * t
    t6 = t4 * t2
    envelope = 1.0 - t6 * (28.0 - t * (48.0 - 21.0 * t))
    theta = math.pi * t
    sines, cosines = {1: jnp.sin(theta)}, {1: jnp.cos(theta)}
    for b in range(2, NB + 1):
        i, j = (b + 1) // 2, b // 2
        sines[b] = sines[i] * cosines[j] + cosines[i] * sines[j]
        cosines[b] = cosines[i] * cosines[j] - sines[i] * sines[j]
    scale = math.sqrt(2.0 / CUTOFF)
    shape = scale * envelope * inv
    if basis_slope is not None:
        envelope_slope = (-168.0 / CUTOFF) * t5 * (1.0 - t) * (1.0 - t)
        shape_slope = scale * inv * (envelope_slope - envelope * inv)
    for b in range(1, NB + 1):
        value = sines[b] * shape
        for half in range(value.shape[0] // 8):
            basis[half, 8 * b - 8 : 8 * b, :] = value[8 * half : 8 * half + 8]
        if basis_slope is not None:
            basis_slope[8 * b - 8 : 8 * b, :] = (
                (b * math.pi / CUTOFF) * cosines[b] * shape + sines[b] * shape_slope
            )
    return inv, ux, uy, uz


CHARGE_SCRATCH = [
    pltpu.VMEM((136, EXT), f32),
    pltpu.VMEM((288, EXT), bf16),
    pltpu.VMEM((16, ATOM), jnp.int32),
    pltpu.VMEM((2, 8 * NB, ATOM), f32),
    pltpu.VMEM((8, 16, ATOM), f32),
    pltpu.VMEM((K, 3 * C, ATOM), f32),
    pltpu.VMEM((K, C, ATOM), f32),
    pltpu.SemaphoreType.DMA((4,)),
]


def charges_kernel(
    left, own, right, low, high, codes, up_wide, in_wide, out_wide, columns, waves_z,
    spread, charge_out, rel, places_out, along, kept,
    table, split, target_ref, basis, harm, radial, up, sems,
):
    own_pos = own[C : C + 8, :]
    weights_x, _ = spline_rows(own_pos[0:1], PLANE0, 8, False)
    weights_y, _ = spline_rows(own_pos[1:2], ROW0, ROW_PAD, False)

    table[:, 0:128] = left[...]
    table[:, 128:384] = own[...]
    table[:, 384:512] = right[...]
    table[:, 512:576] = low[...]
    table[:, 576:640] = high[...]

    mapped = layered(up_wide, table[0:C, :])
    m_high, m_low = halves(mapped)
    split[0:C, :] = m_high.astype(bf16)
    split[C : 2 * C, :] = m_low.astype(bf16)

    lane = lax.broadcasted_iota(jnp.int32, (8, EXT), 1)
    part = lax.broadcasted_iota(jnp.int32, (8, EXT), 0)
    plane = jnp.where(lane < 512, lane >> 7, (lane >> 4) & 3)
    shift_x = jnp.where(plane == 0, -2.0, jnp.where(plane == 3, 2.0, 0.0))
    shift_y = jnp.where(lane >= 576, 16.0, jnp.where(lane >= 512, -16.0, 0.0))
    places = table[C : C + 8, :] + jnp.where(
        part == 0, shift_x, jnp.where(part == 1, shift_y, 0.0)
    )
    places_out[...] = places
    p_high, p_rest = halves(places)
    p_mid, p_low = halves(p_rest)
    split[2 * C : 2 * C + 32, :] = jnp.concatenate(
        [p_high, p_mid, p_low, jnp.zeros_like(p_low)], axis=0
    ).astype(bf16)

    padded = jnp.concatenate(
        [codes[0:HALF, :], codes[0:2, :], codes[HALF:K, :], codes[0:2, :]], axis=0
    )
    target, wrap = edge_targets(padded)
    target_ref[...] = target
    keep = []
    for k in range(K):
        found = dot(split[...], one_hot(target_ref, slot(k), EXT))
        up[k] = found[0:C] + found[C : 2 * C]
        place = found[256:264] + found[264:272] + found[272:280]
        for c in range(3):
            rel[c, slot(k) : slot(k) + 1, :] = place[c : c + 1]
        if k % 3 == 2:
            some = slice(k - 2, k + 1)
            keep.append(pltpu.make_async_copy(up.at[some], kept.at[some], sems.at[k // 3]))
            keep[-1].start()

    rel_x = rel[0] - own_pos[0:1]
    rel_y = rel[1] - own_pos[1:2]
    rel_z = rel[2] - own_pos[2:3] + wrap.astype(f32) * float(NZ)
    spare = (lax.broadcasted_iota(jnp.int32, (16, ATOM), 0) & 7) >= HALF
    rel_x, rel_y, rel_z = (jnp.where(spare, 1.0, x) for x in (rel_x, rel_y, rel_z))
    rel[0], rel[1], rel[2] = rel_x, rel_y, rel_z
    geometry(rel_x, rel_y, rel_z, harm, basis, None)

    for half in range(2):
        before = layered(in_wide, basis[half])
        hidden = before * jax.nn.sigmoid(before)
        for k in range(HALF):
            radial[HALF * half + k] = layered(out_wide, hidden[RH * k : RH * k + RH])

    charge = []
    site = jnp.zeros((8, 128), f32)
    for half in range(2):
        lanes = slice(128 * half, 128 * half + 128)

        def accumulate(step, carry):
            c0 = pl.multiple_of(step * 8, 8)
            block = pl.ds(c0, 8)
            total = [jnp.zeros((8, 128), f32) for _ in range(9)]
            for k in range(K):
                u = up[k, block, lanes]
                total[0] += radial[k, block, lanes] * u
                first = radial[k, pl.ds(c0 + C, 8), lanes] * u
                second = radial[k, pl.ds(c0 + 2 * C, 8), lanes] * u
                for m in range(8):
                    total[1 + m] += (
                        first if m < 3 else second
                    ) * harm[m, slot(k) : slot(k) + 1, lanes]
            for m in range(8):
                along[m, block, lanes] = total[1 + m] * columns[8 if m < 3 else 9, block, :]
            first = sum(total[m] * total[m] for m in range(1, 4))
            second = sum(total[m] * total[m] for m in range(4, 9))
            feature = own[block, lanes]
            return tuple(
                carry[w]
                + columns[4 * w, block, :] * total[0]
                + columns[4 * w + 1, block, :] * first
                + columns[4 * w + 2, block, :] * second
                + columns[4 * w + 3, block, :] * feature
                for w in range(2)
            )

        zero = jnp.zeros((8, 128), f32)
        sites, charges = lax.fori_loop(0, 16, accumulate, (zero, zero), unroll=16)
        site = site + sites
        charge.append(jnp.sum(charges, axis=0, keepdims=True))
    charge = jnp.concatenate(charge, axis=1)
    charge_out[...] = charge

    charged = weights_y * charge
    planes = jnp.concatenate([charged * weights_x[p : p + 1] for p in OWN_PLANES], axis=0)
    top, rest = halves(planes)
    planes = dot_nt(jnp.concatenate([top, rest, top], axis=1).astype(bf16), waves_z[...])
    lane = lax.broadcasted_iota(jnp.int32, (ROW_PAD, 128), 1)
    row = lax.broadcasted_iota(jnp.int32, (ROW_PAD, 128), 0)
    extra = jnp.where(row == SUM_ROW, spread_out(jnp.sum(site), lane), 0.0)
    for g in range(N_GY):
        part = extra
        for i, p in enumerate(OWN_PLANES):
            amount = (16 * (p - g)) % 128
            moved = planes[ROW_PAD * i : ROW_PAD * i + ROW_PAD]
            moved = pltpu.roll(moved, amount, 1) if amount else moved
            part = jnp.where((lane >> 4) == p, moved, part)
        spread[g] = part
    for copy in keep:
        copy.wait()


def y_in_kernel(rows, table, out):
    waves = layered(table, rows[...].reshape(N_GY * ROW_PAD, 128))
    out[:, 0, :] = waves[0:64]
    out[:, 1, :] = waves[64:128]


def x_kernel(planes, x_in, x_out, x_gain, x_square, yz, out):
    sides = jnp.concatenate([planes[:, 0, :], planes[:, 1, :]], axis=1)
    site = jnp.sum(planes[:, 0, SUM_LANE : SUM_LANE + 3])
    waves = layered(x_in, sides)
    filtered = []
    energy = site * (1.0 / (N_GX * N_GY))
    for half in range(2):
        total = jnp.zeros((128, 128), f32)
        for i, p in enumerate(OWN_PLANES):
            block = waves[128 * i : 128 * i + 128, 128 * half : 128 * half + 128]
            total = total + pltpu.roll(block, (128 - 16 * p) % 128, 1)
        square = x_square[...] + yz[0, 2 * half + 1 : 2 * half + 2, :]
        anchor = square == 0.0
        kernel = jnp.where(
            anchor,
            0.0,
            x_gain[...] * yz[0, 2 * half : 2 * half + 1, :] / jnp.where(anchor, 1.0, square),
        )
        shaped = kernel * total
        energy = energy + 0.5 * jnp.sum(shaped * total)
        filtered.append(shaped)
    back = layered(x_out, jnp.concatenate(filtered, axis=1))
    lane = lax.broadcasted_iota(jnp.int32, (64, 128), 1)
    for half in range(2):
        total = spread_out(energy, lane) if half == 0 else jnp.zeros((64, 128), f32)
        for p in range(PLANES):
            block = back[64 * p : 64 * p + 64, 128 * half : 128 * half + 128]
            moved = pltpu.roll(block, 16 * p, 1) if p else block
            total = total + moved
        out[:, half, :] = total


def y_out_kernel(waves, table, out):
    both = jnp.concatenate([waves[:, 0, :], waves[:, 1, :]], axis=0)
    out[...] = layered(table, both).reshape(N_GY, ROW_PAD, 128)


SLOPE_SCRATCH = [
    pltpu.VMEM((1, 8 * NB, ATOM), f32),
    pltpu.VMEM((8 * NB, ATOM), f32),
    pltpu.VMEM((8, 8, ATOM), f32),
    pltpu.VMEM((HALF, 3 * C, ATOM), f32),
    pltpu.VMEM((HALF, 3 * C, ATOM), f32),
    pltpu.VMEM((HALF, 24, ATOM), f32),
    pltpu.VMEM((HALF, C, ATOM), f32),
    pltpu.SemaphoreType.DMA((1,)),
]


def slopes_kernel(
    k0, rel, kept, along, codes, in_wide, out_wide, columns, *refs
):
    scratch = refs[-8:]
    basis, basis_slope, harm, radial, radial_slope, gathered, up, sems = scratch
    before_planes, planes = (refs[0:2], refs[2:4]) if k0 else ((), refs[0:2])
    base = 8 * k0
    for done, plane in zip(before_planes, planes):
        plane[0:base, :] = done[...]
    fetch = pltpu.make_async_copy(kept.at[k0 : k0 + HALF], up, sems.at[0])
    fetch.start()
    first = slot(k0)
    inv, ux, uy, uz = geometry(
        *(rel[c, first : first + 8, :] for c in range(3)), harm, basis, basis_slope
    )
    before = layered(in_wide, basis[0])
    before_slope = layered(in_wide, basis_slope[...])
    gate = jax.nn.sigmoid(before)
    hidden = before * gate
    hidden_slope = gate * (1.0 + before * (1.0 - gate)) * before_slope
    for k in range(HALF):
        radial[k] = layered(out_wide, hidden[RH * k : RH * k + RH])
        radial_slope[k] = layered(out_wide, hidden_slope[RH * k : RH * k + RH])

    fetch.wait()
    for half in range(2):
        spots = slice(128 * half, 128 * half + 128)

        for k in range(HALF):
            total = [jnp.zeros((8, 128), f32) for _ in range(18)]
            shapes = [
                jnp.broadcast_to(harm[m, k : k + 1, spots], (8, 128)) for m in range(8)
            ]
            for block in range(16):
                c0 = 8 * block
                rows = [slice(c0 + C * i, c0 + C * i + 8) for i in range(3)]
                u = up[k, rows[0], spots]
                turn = [along[m, rows[0], spots] for m in range(8)]
                turn_1 = sum(turn[m] * shapes[m] for m in range(3))
                turn_2 = sum(turn[m] * shapes[m] for m in range(3, 8))
                stretch = u * (
                    radial_slope[k, rows[0], spots]
                    + radial_slope[k, rows[1], spots] * turn_1
                    + radial_slope[k, rows[2], spots] * turn_2
                )
                first = radial[k, rows[1], spots] * u
                second = radial[k, rows[2], spots] * u
                for w in range(2):
                    weight = columns[4 * w, rows[0], :]
                    total[9 * w] += weight * stretch
                    first_w = weight * first
                    second_w = weight * second
                    for m in range(8):
                        total[9 * w + 1 + m] += (first_w if m < 3 else second_w) * turn[m]
            sums = [jnp.sum(total[i], axis=0, keepdims=True) for i in range(18)]
            gathered[k, :, spots] = jnp.concatenate(sums + [jnp.zeros((6, 128), f32)], axis=0)

    r3, r5, r15 = math.sqrt(3.0), math.sqrt(5.0), math.sqrt(15.0)
    for w in range(2):
        g = [
            jnp.concatenate(
                [gathered[k, i : i + 1, :] for k in range(HALF)] + [jnp.zeros((2, ATOM), f32)],
                axis=0,
            )
            for i in range(9 * w, 9 * w + 9)
        ]
        vx = r3 * g[1] + r15 * (uy * g[4] + uz * g[7] + ux * g[8])
        vy = r3 * g[2] + r15 * (ux * g[4] + uz * g[5] - uy * g[8])
        vz = r3 * g[3] + r15 * (uy * g[5] + ux * g[7]) + (3.0 * r5) * uz * g[6]
        radial_part = g[0] - (vx * ux + vy * uy + vz * uz) * inv
        for c, (v, along_c) in enumerate(((vx, ux), (vy, uy), (vz, uz))):
            first = base + 8 * (3 * w + c)
            pull = radial_part * along_c + v * inv
            spare = codes[k0 + 2 * c : k0 + 2 * c + 2, :].astype(f32)
            pull = jnp.concatenate([pull[0:HALF], spare if w == 0 else 0.0 * spare], axis=0)
            planes[0][first : first + 8, :] = pull[:, 0:128]
            planes[1][first : first + 8, :] = pull[:, 128:256]


def reach_kernel(places, z_table, out):
    weights, slopes = spline_rows(places[2:3, :], 0, NZ, True)
    both = jnp.concatenate([weights, slopes[:, 128:384]], axis=1)
    high, low = halves(dot(z_table[...], both, highest))
    out[...] = jnp.concatenate([high, low, high], axis=0).astype(bf16)


def final_kernel(
    potential, places, charge, waves, left, lower, upper, right, low, high, forces, energy_out,
    pulls, target_ref,
):
    pulls[:, 0:128] = left[...]
    pulls[:, 128:256] = lower[...]
    pulls[:, 256:384] = upper[...]
    pulls[:, 384:512] = right[...]
    pulls[:, 512:576] = low[...]
    pulls[:, 576:640] = high[...]
    codes = [
        pulls[48 * half + 8 * c + HALF : 48 * half + 8 * c + 8, :]
        for half in range(2)
        for c in range(3)
    ]
    codes = jnp.concatenate(codes, axis=0)
    target_ref[...] = own_targets(codes.astype(jnp.int32))

    mine = slice(128, 384)
    weights_x, slopes_x = spline_rows(places[0:1, :], PLANE0, 8, False)
    weights_y, slopes_y = spline_rows(places[1:2, :], ROW0, ROW_PAD, False)
    lane = lax.broadcasted_iota(jnp.int32, (ROW_PAD, 128), 1)
    energy = jnp.zeros((1, 3), f32)
    for g in range(N_GY):
        energy = energy + potential[g, SUM_ROW : SUM_ROW + 1, SUM_LANE : SUM_LANE + 3]
    energy_out[...] = jnp.sum(energy, axis=1, keepdims=True) * (1.0 / ATOMS_ALL)
    planes = []
    for p in range(PLANES):
        plane = jnp.zeros((ROW_PAD, 128), f32)
        for g in range(N_GY):
            amount = (16 * (g - p)) % 128
            moved = pltpu.roll(potential[g], amount, 1) if amount else potential[g]
            plane = jnp.where((lane >> 4) == g, moved, plane)
        planes.append(plane)
    felt = dot(beside(jnp.concatenate(planes, axis=0)), waves[...])
    phi = jnp.zeros((1, EXT), f32)
    slope = [jnp.zeros((1, ATOM), f32)] * 3
    for p in range(PLANES):
        here = felt[ROW_PAD * p : ROW_PAD * p + ROW_PAD, 0:EXT]
        by_y = jnp.sum(here * weights_y, axis=0, keepdims=True)
        phi = phi + by_y * weights_x[p : p + 1]
        slope[0] = slope[0] + by_y[:, mine] * slopes_x[p : p + 1, mine]
        by_y = jnp.sum(here[:, mine] * slopes_y[:, mine], axis=0, keepdims=True)
        slope[1] = slope[1] + by_y * weights_x[p : p + 1, mine]
        here = felt[ROW_PAD * p : ROW_PAD * p + ROW_PAD, EXT:]
        by_y = jnp.sum(here * weights_y[:, mine], axis=0, keepdims=True)
        slope[2] = slope[2] + by_y * weights_x[p : p + 1, mine]

    total = [
        [
            pulls[i + 8 * c : i + 8 * c + 8, :] + phi * pulls[i + 24 + 8 * c : i + 32 + 8 * c, :]
            for c in range(3)
        ]
        for i in (0, 48)
    ]
    part = lax.broadcasted_iota(jnp.int32, (16, EXT), 0)
    table = jnp.zeros((96, 16), f32)
    for k in range(K):
        rows = jnp.concatenate(
            [total[k // HALF][c][k % HALF : k % HALF + 1, :] for c in range(3)]
            + [jnp.zeros((5, EXT), f32)],
            axis=0,
        )
        target = target_ref[k : k + 1, :]
        here = part == (target >> 4)
        by_row = [
            jnp.where(here, x[c : c + 1, :], 0.0) for x in halves(rows) for c in range(3)
        ]
        by_site = jnp.where(part == (target & 15), 1.0, 0.0).astype(bf16)
        table = table + dot_nt(jnp.concatenate(by_row, axis=0).astype(bf16), by_site)
    table = table[0:48] + table[48:96]
    table = jnp.concatenate([table, jnp.zeros((48, 112), f32)], axis=1)
    for c in range(3):
        ends = []
        for plane in range(2):
            lanes = table[16 * c + 8 * plane : 16 * c + 8 * plane + 1]
            for a in range(1, 8):
                row = 16 * c + 8 * plane + a
                lanes = lanes + pltpu.roll(table[row : row + 1], 16 * a, 1)
            ends.append(lanes)
        forces[c : c + 1, :] = (
            jnp.sum(total[0][c][0:HALF, mine] + total[1][c][0:HALF, mine], axis=0, keepdims=True)
            - jnp.concatenate(ends, axis=1)
            - charge[...] * slope[c]
        )


def call(kernel, outs, scratch, flops, *args, far_in=(), far_out=(), mib=8):
    args = [
        pltpu.with_memory_space_constraint(x, pltpu.HBM) if i in far_in else x
        for i, x in enumerate(args)
    ]
    near, far = pl.BlockSpec(memory_space=pltpu.VMEM), pl.BlockSpec(memory_space=pltpu.HBM)
    out_specs = near
    if isinstance(outs, tuple):
        out_specs = tuple(far if i in far_out else near for i in range(len(outs)))
    return pl.pallas_call(
        kernel,
        out_shape=outs,
        in_specs=[far if i in far_in else near for i in range(len(args))],
        out_specs=out_specs,
        scratch_shapes=scratch,
        compiler_params=pltpu.CompilerParams(vmem_limit_bytes=mib * 1024 * 1024),
        cost_estimate=pl.CostEstimate(flops=flops, bytes_accessed=2000000, transcendentals=0),
    )(*args)


def passed_along(array, axis, by):
    devices = lax.axis_size(axis)
    return lax.ppermute(array, axis, [(i, (i + by) % devices) for i in range(devices)])


def plane_ghosts(lower, upper):
    return passed_along(upper, "gx", 1), passed_along(lower, "gx", -1)


def row_ghosts(*planes):
    low = passed_along(jnp.concatenate([x[:, 112:] for x in planes], axis=1), "gy", 1)
    high = passed_along(jnp.concatenate([x[:, :16] for x in planes], axis=1), "gy", -1)
    return low, high


def struct(*shape, dtype=f32):
    return jax.ShapeDtypeStruct(shape, dtype)


def shards(
    positions, features, neighbours, up_weight, radial_in, radial_out, coupling, mix_weight,
    readout, charge_weight,
):
    table = {name: jnp.asarray(value) for name, value in TABLES.items()}
    own = jnp.concatenate([features, positions, jnp.zeros((5, ATOM), f32)], axis=0)
    lower, upper = own[:, 0:128], own[:, 128:256]
    left, right = plane_ghosts(lower, upper)
    low, high = row_ghosts(left, lower, upper, right)
    waves_z, columns, up_wide, in_wide, out_wide = call(
        prepare_kernel,
        (
            struct(NZ, 3 * ATOM, dtype=bf16),
            struct(10, C, 128),
            struct(C, 3 * C, dtype=bf16),
            struct(HALF * RH, 24 * NB, dtype=bf16),
            struct(3 * C, 3 * RH, dtype=bf16),
        ),
        [pltpu.VMEM((8, C), f32)],
        10**8,
        own,
        coupling,
        mix_weight,
        readout.reshape(1, C),
        charge_weight.reshape(1, C),
        up_weight,
        radial_in.T,
        radial_out.T,
        table["z"],
    )
    device = lax.axis_index("gx") * N_GY + lax.axis_index("gy")
    yz = lax.dynamic_slice(table["yz"], (device, 0, 0), (1, 4, 128))

    spread, charge, rel, places, along, kept = call(
        charges_kernel,
        (
            struct(N_GY, ROW_PAD, 128),
            struct(1, ATOM),
            struct(3, 16, ATOM),
            struct(8, EXT),
            struct(8, C, ATOM),
            pltpu.HBM((K, C, ATOM), f32),
        ),
        CHARGE_SCRATCH,
        10**9,
        left,
        own,
        right,
        low,
        high,
        neighbours,
        up_wide,
        in_wide,
        out_wide,
        columns,
        waves_z,
        far_out=(5,),
        mib=28,
    )
    spread, yz = lax.optimization_barrier((spread, yz))

    def pulls_of(k0, kept, *before):
        return call(
            functools.partial(slopes_kernel, k0),
            (struct(8 * k0 + 48, 128),) * 2,
            SLOPE_SCRATCH,
            2 * 10**9,
            rel,
            kept,
            along,
            neighbours,
            in_wide,
            out_wide,
            columns,
            *before,
            far_in=(1,),
            mib=28,
        )

    rows = lax.all_to_all(spread, "gy", split_axis=0, concat_axis=0, tiled=True)
    pulls = pulls_of(0, kept)
    rows, *pulls = lax.optimization_barrier((rows, *pulls))
    waves = call(y_in_kernel, struct(N_GX, 2, 128), [], 10**7, rows, table["y_in"])
    waves, kept = lax.optimization_barrier((waves, kept))
    planes = lax.all_to_all(waves, "gx", split_axis=0, concat_axis=0, tiled=True)
    lower, upper = pulls_of(HALF, kept, *pulls)
    planes, _ = lax.optimization_barrier((planes, lower))
    waves = call(
        x_kernel,
        struct(N_GX, 2, 128),
        [],
        10**7,
        planes,
        table["x_in"],
        table["x_out"],
        table["x_gain"],
        table["x_square"],
        yz,
    )
    reach = call(reach_kernel, struct(3 * NZ, EXT + ATOM, dtype=bf16), [], 10**8, places, table["z"])
    waves = lax.all_to_all(waves, "gx", split_axis=0, concat_axis=0, tiled=True)
    left, right = plane_ghosts(lower, upper)
    waves, left, right = lax.optimization_barrier((waves, left, right))
    low, high = row_ghosts(left, lower, upper, right)
    rows = call(y_out_kernel, struct(N_GY, ROW_PAD, 128), [], 10**7, waves, table["y_out"])
    potential = lax.all_to_all(rows, "gy", split_axis=0, concat_axis=0, tiled=True)
    forces, energy = call(
        final_kernel,
        (struct(3, ATOM), struct(1, 1)),
        [pltpu.VMEM((96, EXT), f32), pltpu.VMEM((K, EXT), jnp.int32)],
        10**9,
        potential,
        places,
        charge,
        reach,
        left,
        lower,
        upper,
        right,
        low,
        high,
    )
    return (forces, energy.reshape(()))


def solution(mesh):
    placed = (P(None, ("gx", "gy")),) * 3 + (P(),) * 7
    return jax.shard_map(
        shards, mesh=mesh, in_specs=placed, out_specs=(P(None, ("gx", "gy")), P()), check_vma=False
    )
```
